256 devices in a mesh: loop: 8 (over x_lo, y), dp: 32 (over x_hi, z, core).
Axes of the slice: x: 4 (x_hi: 2, x_lo: 2; x = x_hi * 2 + x_lo), y: 4, z: 8, core: 2. Of those that a mesh axis runs over, the one named last changes fastest.
Arguments:
- residual: bfloat16 [12288, 1024], P('dp', 'loop'), may hold values from -6 to 6
- targets: bfloat16 [12288, 2, 1024], P('dp'), may hold values from -6 to 6
- counts: int32 [32], P('dp'), may hold values from 1 to 384, 6144 in all
- enc_weight: bfloat16 [1024, 16384], P('dp', 'loop'), may hold values from -0.1875 to 0.1875
- enc_bias: float32 [16384], P('loop'), may hold values from -3 to 3
- dec_weight: bfloat16 [16384, 2, 1024], P(('loop', 'dp')), may hold values from -0.046875 to 0.046875
Outputs:
- mean_error: float32 [], replicated
- enc_grad: float32 [1024, 16384], P('dp', 'loop')
- bias_grad: float32 [16384], P('loop')
- dec_grad: float32 [16384, 2, 1024], P(('loop', 'dp'))
The draws below stay inside these ranges and needn't reach their ends.
Inputs may be any that keep to these rules, and one draw needn't show every extreme that they name: The 32 counts sum to 6144, and the largest is 384.
All inputs are finite; a program needn't handle non-finite values. No bound on the sum of `counts` on one device may be relied on, other than what follows from the above.
Results may differ from the reference program's by a relative error of at most 0.022.
Values may be sent and summed in bfloat16 or wider, within the bound.
A program may use at most 128 MiB of HBM per device.

```python
import math
import jax
import jax.numpy as jnp
import numpy as np
from jax import lax

D = 1024
L = 16384
TARGETS = 2
TOK_DEV = 384
TOKENS = 12288
TOTAL_ROWS = 6144
N_DP = 32


def block_levels(stream_key, extent, cuts, smallest, high):
    def one(dim, blocks):
        heights = jax.random.uniform(jax.random.fold_in(jax.random.fold_in(stream_key, 6), dim), (blocks,), jnp.float32, smallest / len(cuts), high / len(cuts))
        return jnp.repeat(jnp.exp(heights), extent[dim] // blocks).reshape((-1,) + (1,) * (len(extent) - dim - 1))

    gain = one(*cuts[0])
    for cut in cuts[1:]:
        gain = gain * one(*cut)
    return gain


def length_profile(number_of, total, most, lean):
    weights = [(1 << 20) // math.isqrt(grade ** lean) + 1 for grade in range(2, number_of + 1)]
    rest, given = total - most - (number_of - 1), [1] * (number_of - 1)
    while rest > 0:
        candidates = [i for i in range(number_of - 1) if given[i] < most]
        pool, budget = sum([weights[i] for i in candidates]), rest
        for i in candidates:
            addition = min(most - given[i], max(1, budget * weights[i] // pool), rest)
            given[i] = given[i] + addition
            rest = rest - addition
    return np.array([most] + given)


def ragged(stream_key, count, total, reach, slope):
    if count == 2:
        one = jax.random.randint(stream_key, (), max(1, total - reach), min(reach, total - 1) + 1)
        return jnp.stack([one, total - one])
    sizes = jnp.asarray(length_profile(count, total, reach, slope), jnp.int32)
    couples = (count - 1) // 2
    source_of, receiver = sizes[1:1 + 2 * couples:2], sizes[2:2 + 2 * couples:2]
    margin = jnp.minimum(source_of - 1, reach - receiver)
    shifted = jax.random.randint(jax.random.fold_in(stream_key, 1), (couples,), 0, 1 << 20) % (margin + 1)
    sizes = sizes.at[1:1 + 2 * couples:2].set(source_of - shifted).at[2:2 + 2 * couples:2].set(receiver + shifted)
    return sizes[jax.random.permutation(jax.random.fold_in(stream_key, 2), count)]


def centred(stream_key, extent, deviation, reach, cuts=(), kind=jnp.bfloat16):
    gain = block_levels(stream_key, extent, cuts, -0.22, 0.18) if cuts else 1.0
    result = jax.random.normal(stream_key, extent, jnp.float32) * deviation * gain
    return jnp.minimum(jnp.maximum(result, -reach), reach).astype(kind)


def setup_inputs(seed: int = 0) -> dict:
    splits = jax.random.split(jax.random.key(seed), 7)
    residual = centred(splits[0], (TOKENS, D), 1.0, 6.0, ((0, 32), (1, 8)))
    targets = centred(splits[1], (TOKENS, TARGETS, D), 1.0, 6.0, ((0, 32),))
    counts = ragged(splits[2], N_DP, TOTAL_ROWS, TOK_DEV, 2).astype(jnp.int32)
    enc_weight = centred(splits[3], (D, L), D ** -0.5, 0.1875, ((0, 32), (1, 8)))
    enc_bias = centred(splits[4], (L,), 0.5, 3.0, ((0, 8),), jnp.float32)
    dec_weight = centred(splits[5], (L, TARGETS, D), L ** -0.5, 0.046875, ((0, 256),))
    return dict(residual=residual, targets=targets, counts=counts, enc_weight=enc_weight, enc_bias=enc_bias, dec_weight=dec_weight)


def narrow_sum(value):
    return lax.optimization_barrier(value.astype(jnp.bfloat16)).astype(jnp.float32)

def reference(residual, targets, counts, enc_weight, enc_bias, dec_weight):
    d_model = residual.shape[1]
    latents = enc_weight.shape[1]
    parts = targets.shape[1]
    highest = lax.Precision.HIGHEST
    enc_wide = enc_weight.astype(jnp.float32)
    dec_flat = dec_weight.reshape(latents, parts * d_model).astype(jnp.float32)
    grad_scale = 2.0 / math.sqrt(TOTAL_ROWS)
    features = residual.reshape(N_DP, TOK_DEV, d_model)
    wanted = targets.reshape(N_DP, TOK_DEV, parts * d_model)

    def block_step(carry, inputs):
        sq_sum, enc_acc, bias_acc, dec_acc = carry
        feats, goal, limit = inputs
        feats_wide = feats.astype(jnp.float32)
        preact = jnp.dot(feats_wide, enc_wide, precision=highest) + enc_bias
        active = jnp.maximum(preact, 0.0).astype(jnp.bfloat16)
        active_wide = active.astype(jnp.float32)
        rebuilt = jnp.dot(active_wide, dec_flat, precision=highest)
        row_valid = (jnp.arange(TOK_DEV, dtype=jnp.int32) < limit).astype(jnp.float32)[:, None]
        misfit = (rebuilt - goal.astype(jnp.float32)) * row_valid
        sq_sum = sq_sum + jnp.sum(misfit * misfit)
        out_grad = (grad_scale * misfit).astype(jnp.bfloat16).astype(jnp.float32)
        backprop = jnp.dot(out_grad, dec_flat.T, precision=highest)
        pre_grad = jnp.where(preact > 0, backprop, 0.0)
        bias_acc = bias_acc + lax.optimization_barrier(jnp.sum(pre_grad, axis=0))
        pre_narrow = pre_grad.astype(jnp.bfloat16).astype(jnp.float32)
        dec_acc = dec_acc + narrow_sum(jnp.dot(active_wide.T, out_grad, precision=highest))
        enc_acc = enc_acc + narrow_sum(jnp.dot(feats_wide.T, pre_narrow, precision=highest))
        return ((sq_sum, enc_acc, bias_acc, dec_acc), None)
    init = (jnp.zeros((), jnp.float32), jnp.zeros((d_model, latents), jnp.float32), jnp.zeros((latents,), jnp.float32), jnp.zeros((latents, parts * d_model), jnp.float32))
    final, _ = lax.scan(block_step, init, (features, wanted, counts))
    sq_sum, enc_acc, bias_acc, dec_acc = final
    mean_error = sq_sum / (TOTAL_ROWS * parts * d_model)
    return (mean_error, enc_acc, bias_acc, dec_acc.reshape(latents, parts, d_model))
```

```python
import math

import jax
import jax.numpy as jnp
from jax import lax
from jax.experimental import pallas as pl
from jax.experimental.pallas import tpu as pltpu
from jax.sharding import PartitionSpec as P

MESH = pl.DeviceIdType.MESH
BF16 = jnp.bfloat16
F32 = jnp.float32


def place():
    loop, dp = lax.axis_index("loop"), lax.axis_index("dp")
    x = (dp // 16) * 2 + loop // 4
    return x, loop % 4, (dp % 16) // 2, dp % 2


def ident(x, y, z, core):
    return ((x % 2) * 4 + y, (x // 2) * 16 + z * 2 + core)


def greet(peers):
    barrier = pltpu.get_barrier_semaphore()
    for peer in peers:
        pl.semaphore_signal(barrier, inc=1, device_id=peer, device_id_type=MESH)
    pl.semaphore_wait(barrier, len(peers))


def remote(src, dst, send, recv, peer):
    return pltpu.make_async_remote_copy(
        src_ref=src, dst_ref=dst, send_sem=send, recv_sem=recv, device_id=peer, device_id_type=MESH
    )


class Gather:
    def __init__(self, n, at, right, left, whole, half, sems):
        self.n, self.at, self.right, self.left = n, at, right, left
        self.whole, self.half, self.sems = whole, half, sems
        self.steps = []

    def step(self):
        s = len(self.steps)
        if s:
            for copy in self.steps[-1]:
                copy.wait_recv()
        if s == self.n // 2:
            return
        pair = []
        for side, peer in ((0, self.right), (1, self.left)):
            block = (self.at + (self.n - s if side == 0 else s)) % self.n
            ref = self.half(block, side) if s == self.n // 2 - 1 else self.whole(block)
            copy = remote(ref, ref, self.sems.at[0, side, s], self.sems.at[1, side, s], peer)
            copy.start()
            pair.append(copy)
        self.steps.append(pair)

    def drain(self):
        for pair in self.steps:
            for copy in pair:
                copy.wait_send()


def add_into(ref, other):
    ref[...] = (ref[...].astype(F32) + other[...].astype(F32)).astype(BF16)


class Reduce:
    def __init__(self, n, at, right, left, whole, half, landed, sems):
        self.n, self.at, self.right, self.left = n, at, right, left
        self.whole, self.half, self.landed, self.sems = whole, half, landed, sems
        self.steps = []

    def step(self):
        s = len(self.steps)
        depth = self.n // 2
        pair = []
        for side, peer in ((0, self.right), (1, self.left)):
            if s:
                self.steps[-1][side].wait_recv()
            if s == depth:
                continue
            far = depth - s
            block = (self.at + (far if side == 0 else self.n - far)) % self.n
            if s:
                part = self.half(block, side) if s == 1 else self.whole(block)
                add_into(part, self.landed[side][s - 1])
            ref = self.half(block, side) if s == 0 else self.whole(block)
            copy = remote(ref, self.landed[side][s], self.sems.at[0, side, s], self.sems.at[1, side, s], peer)
            copy.start()
            pair.append(copy)
        if s < depth:
            self.steps.append(pair)

    def drain(self):
        for pair in self.steps:
            for copy in pair:
                copy.wait_send()


def gather_kernel(res, enc, dec, res_all, enc_all, dec_all, ysem, xsem, esem, dsem, qsem, csem, lsem):
    x, y, z, core = place()
    x_hi = x // 2
    up, down = ident(x, y, (z + 1) % 8, core), ident(x, y, (z + 7) % 8, core)
    east, west = ident((x + 1) % 4, y, z, core), ident((x + 3) % 4, y, z, core)
    north, south = ident(x, (y + 1) % 4, z, core), ident(x, (y + 3) % 4, z, core)
    other = ident(x, y, z, 1 - core)
    quad = [(1 - x_hi, core), (x_hi, 1 - core), (1 - x_hi, 1 - core)]
    quad_ids = [ident((x + 2) % 4, y, z, core), other, ident((x + 2) % 4, y, z, 1 - core)]
    greet([up, down, east, west, north, south] + quad_ids)

    def cols(block, width):
        return pl.ds(pl.multiple_of(block * width, width), width)

    def mine(xx, yy):
        return res_all.at[core, xx // 2, :, cols((xx % 2) * 4 + yy, 128)]

    local = [
        pltpu.make_async_copy(res, mine(x, y), lsem.at[0]),
        pltpu.make_async_copy(enc.at[x_hi, core], enc_all.at[x_hi, z, core], lsem.at[1]),
        pltpu.make_async_copy(dec, dec_all.at[z], lsem.at[2]),
    ]
    for copy in local:
        copy.start()
    swap = []
    for i, (q, peer) in enumerate(zip(quad, quad_ids)):
        copy = remote(enc.at[q[0], q[1]], enc_all.at[x_hi, z, core], qsem.at[0, i], qsem.at[1, i], peer)
        copy.start()
        swap.append(copy)
    for copy in local:
        copy.wait()
    ring_y = Gather(
        4, y, north, south, lambda b: mine(x, b),
        lambda b, h: res_all.at[core, x_hi, pl.ds(192 * h, 192), cols((x % 2) * 4 + b, 128)], ysem,
    )
    ring_x = Gather(
        4, x, east, west, lambda b: res_all.at[core, b // 2, :, cols(b % 2, 512)],
        lambda b, h: res_all.at[core, b // 2, pl.ds(192 * h, 192), cols(b % 2, 512)], xsem,
    )
    ring_e = Gather(8, z, up, down, lambda b: enc_all.at[:, b], lambda b, h: enc_all.at[h, b], esem)
    ring_d = Gather(8, z, up, down, lambda b: dec_all.at[b], lambda b, h: dec_all.at[b, pl.ds(32 * h, 32)], dsem)
    ring_y.step()
    for copy in swap:
        copy.wait_recv()
    ring_e.step()
    ring_d.step()
    ring_y.step()
    ring_y.step()
    ring_x.step()
    ring_e.step()
    ring_d.step()
    ring_x.step()
    ring_e.step()
    ring_d.step()
    ring_x.step()
    cross = remote(res_all.at[core], res_all.at[core], csem.at[0], csem.at[1], other)
    cross.start()
    ring_e.step()
    ring_d.step()
    ring_e.step()
    ring_d.step()
    cross.wait()
    for copy in swap:
        copy.wait_send()
    for ring in (ring_y, ring_x, ring_e, ring_d):
        ring.drain()


def exchange_kernel(
    scale, part, goal, valid, grads, sq, crossed,
    a1, a2, b1, b2, c1, c2, d1, d2, mid_a, mid_b,
    asem, bsem, csem, dsem, esem, fsem, gsem, hsem, osem,
):
    x, y, z, core = place()
    east, west = ident((x + 1) % 4, y, z, core), ident((x + 3) % 4, y, z, core)
    north, south = ident(x, (y + 1) % 4, z, core), ident(x, (y + 3) % 4, z, core)
    other = ident(x, y, z, 1 - core)
    greet([east, west, north, south, other])
    lo, hi = pl.ds(0, 1024), pl.ds(1024, 1024)
    cross = remote(part.at[1 - core], crossed, osem.at[0, 0], osem.at[0, 1], other)
    cross.start()
    cross.wait()
    mine = part.at[core]

    def total(i, _):
        add_into(mine.at[i // 4, i % 4], crossed.at[i // 4, i % 4])
        return 0

    lax.fori_loop(0, 16, total, 0)
    red_a = Reduce(
        4, x, east, west, lambda b: mine.at[b, :, :, lo], lambda b, h: mine.at[b, pl.ds(2 * h, 2), :, lo],
        [[a1.at[s], a2.at[s]] for s in range(2)], asem,
    )
    red_b = Reduce(
        4, y, north, south, lambda b: mine.at[:, b, :, hi], lambda b, h: mine.at[pl.ds(2 * h, 2), b, :, hi],
        [[b1.at[s], b2.at[s]] for s in range(2)], bsem,
    )
    for _ in range(3):
        red_a.step()
        red_b.step()
    mid_a[...] = (mine[x, :, :, lo].astype(F32) + a2[0].astype(F32) + a2[1].astype(F32)).astype(BF16)
    red_c = Reduce(
        4, y, north, south, lambda b: mid_a.at[b], lambda b, h: mid_a.at[b, :, pl.ds(512 * h, 512)],
        [[c1.at[s], c2.at[s]] for s in range(2)], csem,
    )
    red_c.step()
    mid_b[...] = (mine[:, y, :, hi].astype(F32) + b2[0].astype(F32) + b2[1].astype(F32)).astype(BF16)
    red_d = Reduce(
        4, x, east, west, lambda b: mid_b.at[b], lambda b, h: mid_b.at[b, :, pl.ds(512 * h, 512)],
        [[d1.at[s], d2.at[s]] for s in range(2)], dsem,
    )
    red_d.step()
    for _ in range(2):
        red_c.step()
        red_d.step()
    out = grads.at[core]
    ok = valid[:, 0:1]
    rebuilt = mid_a[y].astype(F32) + c2[0].astype(F32) + c2[1].astype(F32)
    miss = (rebuilt - goal[:, lo].astype(F32)) * ok
    out[x, y, :, lo] = (scale * miss).astype(BF16)
    squares = jnp.sum(miss * miss, axis=0, keepdims=True)
    ring_c = Gather(
        4, y, north, south, lambda b: out.at[x, b, :, lo], lambda b, h: out.at[x, b, :, pl.ds(512 * h, 512)], esem
    )
    ring_c.step()
    rebuilt = mid_b[x].astype(F32) + d2[0].astype(F32) + d2[1].astype(F32)
    miss = (rebuilt - goal[:, hi].astype(F32)) * ok
    out[x, y, :, hi] = (scale * miss).astype(BF16)
    squares = squares + jnp.sum(miss * miss, axis=0, keepdims=True)
    ring_d = Gather(
        4, x, east, west, lambda b: out.at[b, y, :, hi],
        lambda b, h: out.at[b, y, :, pl.ds(1024 + 512 * h, 512)], fsem,
    )
    ring_d.step()
    sq[...] = squares
    for _ in range(2):
        ring_c.step()
        ring_d.step()
    ring_a = Gather(
        4, x, east, west, lambda b: out.at[b, :, :, lo], lambda b, h: out.at[b, pl.ds(2 * h, 2), :, lo], gsem
    )
    ring_b = Gather(
        4, y, north, south, lambda b: out.at[:, b, :, hi], lambda b, h: out.at[pl.ds(2 * h, 2), b, :, hi], hsem
    )
    for _ in range(3):
        ring_a.step()
        ring_b.step()
    back = remote(out, out, osem.at[1, 0], osem.at[1, 1], other)
    back.start()
    for ring in (red_a, red_b, red_c, red_d, ring_a, ring_b, ring_c, ring_d):
        ring.drain()
    back.wait()


def scatter_kernel(dec, enc, dec_out, enc_out, d1, dn, e1, en, dsem, esem, esum, qsem, lsem):
    x, y, z, core = place()
    x_hi = x // 2
    up, down = ident(x, y, (z + 1) % 8, core), ident(x, y, (z + 7) % 8, core)
    quad = [(1 - x_hi, core), (x_hi, 1 - core), (1 - x_hi, 1 - core)]
    quad_ids = [
        ident((x + 2) % 4, y, z, core), ident(x, y, z, 1 - core), ident((x + 2) % 4, y, z, 1 - core)
    ]
    greet([up, down] + quad_ids)
    red_d = Reduce(
        8, z, up, down, lambda b: dec.at[b], lambda b, h: dec.at[b, pl.ds(32 * h, 32)],
        [[d1.at[s], dn.at[s, 0], dn.at[s, 1], dn.at[s, 2]] for s in range(2)], dsem,
    )
    red_e = Reduce(
        8, z, up, down, lambda b: enc.at[:, b], lambda b, h: enc.at[h, b],
        [[e1.at[s], en.at[s, 0], en.at[s, 1], en.at[s, 2]] for s in range(2)], esem,
    )
    for _ in range(5):
        red_e.step()
        red_d.step()
    esum[...] = enc[:, z].astype(F32) + en[0, 2].astype(F32) + en[1, 2].astype(F32)
    keep = pltpu.make_async_copy(esum.at[x_hi, core], enc_out.at[x_hi, core], lsem.at[0])
    keep.start()
    swap = []
    for i, (q, peer) in enumerate(zip(quad, quad_ids)):
        copy = remote(esum.at[q[0], q[1]], enc_out.at[x_hi, core], qsem.at[0, i], qsem.at[1, i], peer)
        copy.start()
        swap.append(copy)
    dec_out[...] = dec[z].astype(F32) + dn[0, 2].astype(F32) + dn[1, 2].astype(F32)
    keep.wait()
    for copy in swap:
        copy.wait()
    red_d.drain()
    red_e.drain()


VM = pl.BlockSpec(memory_space=pltpu.VMEM)


def dmas(*shape):
    return pltpu.SemaphoreType.DMA(shape)


def params(ident):
    return pltpu.CompilerParams(collective_id=ident, has_side_effects=True, vmem_limit_bytes=56 << 20)


def shape(*dims, dtype=BF16):
    return jax.ShapeDtypeStruct(dims, dtype)


def shards(residual, targets, counts, enc_weight, enc_bias, dec_weight):
    loop, dp = lax.axis_index("loop"), lax.axis_index("dp")
    x_hi, core = dp // 16, dp % 2
    enc_quad = enc_weight.reshape(32, 2, 8, 2, 64).transpose(1, 3, 0, 2, 4).reshape(2, 2, 32, 512)
    res_all, enc_all, dec_all = pl.pallas_call(
        gather_kernel,
        out_shape=(shape(2, 2, 384, 1024), shape(2, 8, 2, 32, 512), shape(8, 64, 2048)),
        in_specs=[VM] * 3,
        out_specs=(VM,) * 3,
        scratch_shapes=[dmas(2, 2, 2), dmas(2, 2, 2), dmas(2, 2, 4), dmas(2, 2, 4), dmas(2, 3), dmas(2), dmas(3)],
        compiler_params=params(1),
    )(residual, enc_quad, dec_weight.reshape(64, 2048))
    feats = res_all.reshape(1536, 1024)
    enc = enc_all.reshape(1024, 512)
    dec = dec_all.reshape(512, 2048)
    bias = lax.dynamic_index_in_dim(
        enc_bias.reshape(2, 8, 2, 64).transpose(0, 2, 1, 3).reshape(4, 512), x_hi * 2 + core, 0, False
    )
    preact = jnp.dot(feats, enc, preferred_element_type=F32) + bias[None, :]
    active = jnp.maximum(preact, 0.0).astype(BF16)
    part = jnp.dot(active, dec, preferred_element_type=F32).astype(BF16)
    goal = lax.dynamic_slice_in_dim(targets, loop * 48, 48, 0).reshape(48, 2048)
    rows = loop * 48 + lax.iota(jnp.int32, 48)
    valid = jnp.broadcast_to((rows < counts[0]).astype(F32)[:, None], (48, 128))
    total_rows = 32 * 384 // 2
    quarter = (2, 2, 48, 1024)
    whole = (2, 4, 48, 1024)
    grads, sq = pl.pallas_call(
        lambda *refs: exchange_kernel(2.0 / math.sqrt(total_rows), *refs),
        out_shape=(shape(2, 4, 4, 48, 2048), shape(1, 1024, dtype=F32)),
        in_specs=[VM] * 3,
        out_specs=(VM,) * 2,
        scratch_shapes=[
            pltpu.VMEM((4, 4, 48, 2048), BF16),
            pltpu.VMEM(quarter, BF16), pltpu.VMEM(whole, BF16),
            pltpu.VMEM(quarter, BF16), pltpu.VMEM(whole, BF16),
            pltpu.VMEM((2, 48, 512), BF16), pltpu.VMEM((2, 48, 1024), BF16),
            pltpu.VMEM((2, 48, 512), BF16), pltpu.VMEM((2, 48, 1024), BF16),
            pltpu.VMEM((4, 48, 1024), BF16), pltpu.VMEM((4, 48, 1024), BF16),
        ] + [dmas(2, 2, 2)] * 8 + [dmas(2, 2)],
        compiler_params=params(2),
    )(part.reshape(2, 4, 4, 48, 2048), goal, valid)
    mean_error = lax.psum(jnp.sum(sq), ("loop", "dp")) / (total_rows * 2048)
    grads = grads.reshape(1536, 2048)
    backprop = lax.dot_general(grads, dec, (((1,), (1,)), ((), ())), preferred_element_type=F32)
    pre_grad = jnp.where(preact > 0, backprop, 0.0)
    bias_part = jnp.zeros((4, 512), F32).at[x_hi * 2 + core].set(jnp.sum(pre_grad, axis=0))
    bias_grad = lax.psum(bias_part, "dp").reshape(2, 2, 8, 64).transpose(0, 2, 1, 3).reshape(2048)
    pre_narrow = pre_grad.astype(BF16)
    dec_prod = lax.dot_general(active, grads, (((0,), (0,)), ((), ())), preferred_element_type=F32).astype(BF16)
    enc_prod = lax.dot_general(feats, pre_narrow, (((0,), (0,)), ((), ())), preferred_element_type=F32).astype(BF16)
    dec_grad, enc_grad = pl.pallas_call(
        scatter_kernel,
        out_shape=(shape(64, 2048, dtype=F32), shape(2, 2, 32, 512, dtype=F32)),
        in_specs=[VM] * 2,
        out_specs=(VM,) * 2,
        scratch_shapes=[
            pltpu.VMEM((2, 32, 2048), BF16), pltpu.VMEM((2, 3, 64, 2048), BF16),
            pltpu.VMEM((2, 2, 32, 512), BF16), pltpu.VMEM((2, 3, 2, 2, 32, 512), BF16),
            dmas(2, 2, 4), dmas(2, 2, 4), pltpu.VMEM((2, 2, 32, 512), F32), dmas(2, 3), dmas(1),
        ],
        compiler_params=params(3),
    )(dec_prod.reshape(8, 64, 2048), enc_prod.reshape(2, 8, 2, 32, 512))
    enc_grad = enc_grad.reshape(2, 2, 32, 8, 64).transpose(2, 0, 3, 1, 4).reshape(32, 2048)
    return mean_error, enc_grad, bias_grad, dec_grad.reshape(64, 2, 1024)


def solution(mesh):
    placed = (
        P("dp", "loop"),
        P("dp", None, None),
        P("dp"),
        P("dp", "loop"),
        P("loop"),
        P(("loop", "dp"), None, None),
    )
    return jax.shard_map(
        shards,
        mesh=mesh,
        in_specs=placed,
        out_specs=(P(), P("dp", "loop"), P("loop"), P(("loop", "dp"), None, None)),
        check_vma=False,
    )
```

```python
import math

import jax
import jax.numpy as jnp
from jax import lax
from jax.experimental import pallas as pl
from jax.experimental.pallas import tpu as pltpu
from jax.sharding import PartitionSpec as P

MESH = pl.DeviceIdType.MESH
BF16 = jnp.bfloat16
F32 = jnp.float32


def place():
    loop, dp = lax.axis_index("loop"), lax.axis_index("dp")
    x = (dp // 16) * 2 + loop // 4
    return x, loop % 4, (dp % 16) // 2, dp % 2


def ident(x, y, z, core):
    return ((x % 2) * 4 + y, (x // 2) * 16 + z * 2 + core)


def greet(peers):
    barrier = pltpu.get_barrier_semaphore()
    for peer in peers:
        pl.semaphore_signal(barrier, inc=1, device_id=peer, device_id_type=MESH)
    pl.semaphore_wait(barrier, len(peers))


def remote(src, dst, send, recv, peer):
    return pltpu.make_async_remote_copy(
        src_ref=src, dst_ref=dst, send_sem=send, recv_sem=recv, device_id=peer, device_id_type=MESH
    )


class Gather:
    def __init__(self, n, at, right, left, whole, half, sems):
        self.n, self.at, self.right, self.left = n, at, right, left
        self.whole, self.half, self.sems = whole, half, sems
        self.steps = []

    def step(self):
        s = len(self.steps)
        if s:
            for copy in self.steps[-1]:
                copy.wait_recv()
        if s == self.n // 2:
            return
        pair = []
        for side, peer in ((0, self.right), (1, self.left)):
            block = (self.at + (self.n - s if side == 0 else s)) % self.n
            last = s == self.n // 2 - 1
            if last and self.half is None and side == 1:
                continue
            ref = self.half(block, side) if last and self.half is not None else self.whole(block)
            copy = remote(ref, ref, self.sems.at[0, side, s], self.sems.at[1, side, s], peer)
            copy.start()
            pair.append(copy)
        self.steps.append(pair)

    def drain(self):
        for pair in self.steps:
            for copy in pair:
                copy.wait_send()


def add_into(ref, other):
    ref[...] = (ref[...].astype(F32) + other[...].astype(F32)).astype(BF16)


class Reduce:
    def __init__(self, n, at, right, left, whole, half, landed, sems):
        self.n, self.at, self.right, self.left = n, at, right, left
        self.whole, self.half, self.landed, self.sems = whole, half, landed, sems
        self.steps = []

    def step(self):
        s = len(self.steps)
        depth = self.n // 2
        pair = []
        for side, peer in ((0, self.right), (1, self.left)):
            if s:
                self.steps[-1][side].wait_recv()
            if s == depth:
                continue
            far = depth - s
            block = (self.at + (far if side == 0 else self.n - far)) % self.n
            if s:
                part = self.half(block, side) if s == 1 else self.whole(block)
                add_into(part, self.landed[side][s - 1])
            ref = self.half(block, side) if s == 0 else self.whole(block)
            copy = remote(ref, self.landed[side][s], self.sems.at[0, side, s], self.sems.at[1, side, s], peer)
            copy.start()
            pair.append(copy)
        if s < depth:
            self.steps.append(pair)

    def drain(self):
        for pair in self.steps:
            for copy in pair:
                copy.wait_send()


def dot(a, b, dims=((1,), (0,))):
    return lax.dot_general(a, b, (dims, ((), ())), preferred_element_type=F32)


def step_kernel(
    scale, res, enc, dec, bias, goal, valid, dec_out, enc_out, bias_out, sq_out,
    res_all, enc_all, dec_all, pre, active, act_t, res_t, sent, crossed, mine, grads,
    a1, a2, b1, b2, c1, c2, d1, d2, mid_a, mid_b, back, narrow, dec_prod, enc_prod,
    dr1, drn, er1, ern, esum, squares, sq_y, sq_x, sq_c, small, small_sum,
    ysem, xsem, esem, dsem, qsem, csem, lsem, psem, bsem, osem, sysem, sxsem, scsem,
    dsem2, esem2, msem, q2sem, q3sem,
):
    x, y, z, core = place()
    x_hi = x // 2
    up, down = ident(x, y, (z + 1) % 8, core), ident(x, y, (z + 7) % 8, core)
    east, west = ident((x + 1) % 4, y, z, core), ident((x + 3) % 4, y, z, core)
    north, south = ident(x, (y + 1) % 4, z, core), ident(x, (y + 3) % 4, z, core)
    other = ident(x, y, z, 1 - core)
    quad = [(1 - x_hi, core), (x_hi, 1 - core), (1 - x_hi, 1 - core)]
    quad_ids = [ident((x + 2) % 4, y, z, core), other, ident((x + 2) % 4, y, z, 1 - core)]
    greet([up, down, east, west, north, south] + quad_ids)
    drains = []

    def cols(block, width):
        return pl.ds(pl.multiple_of(block * width, width), width)

    def feature(xx, yy):
        return res_all.at[core, xx // 2, :, cols((xx % 2) * 4 + yy, 128)]

    local = [
        pltpu.make_async_copy(res, feature(x, y), lsem.at[0]),
        pltpu.make_async_copy(enc.at[x_hi, core], enc_all.at[x_hi, z, core], lsem.at[1]),
        pltpu.make_async_copy(dec, dec_all.at[:, z], lsem.at[2]),
    ]
    for copy in local:
        copy.start()
    swap = []
    for i, (q, peer) in enumerate(zip(quad, quad_ids)):
        copy = remote(enc.at[q[0], q[1]], enc_all.at[x_hi, z, core], qsem.at[0, i], qsem.at[1, i], peer)
        copy.start()
        swap.append(copy)
    for copy in local:
        copy.wait()
    ring_y = Gather(
        4, y, north, south, lambda b: feature(x, b),
        lambda b, h: res_all.at[core, x_hi, pl.ds(192 * h, 192), cols((x % 2) * 4 + b, 128)], ysem,
    )
    ring_x = Gather(
        4, x, east, west, lambda b: res_all.at[core, b // 2, :, cols(b % 2, 512)],
        lambda b, h: res_all.at[core, b // 2, pl.ds(192 * h, 192), cols(b % 2, 512)], xsem,
    )
    ring_e = Gather(8, z, up, down, lambda b: enc_all.at[:, b], lambda b, h: enc_all.at[h, b], esem)
    ring_d = [
        Gather(
            8, z, up, down, lambda b, t=t: dec_all.at[t, b],
            lambda b, h, t=t: dec_all.at[t, b, pl.ds(32 * h, 32)], dsem.at[t],
        )
        for t in range(2)
    ]
    drains += [ring_y, ring_x, ring_e] + ring_d
    ring_y.step()
    for copy in swap:
        copy.wait_recv()
    ring_e.step()
    ring_d[0].step()
    ring_y.step()
    ring_y.step()
    ring_x.step()
    ring_e.step()
    ring_d[0].step()
    ring_x.step()
    ring_e.step()
    ring_d[0].step()
    ring_e.step()
    ring_d[1].step()
    ring_x.step()
    cross = remote(res_all.at[core], res_all.at[core], csem.at[0], csem.at[1], other)
    cross.start()
    ring_d[0].step()
    ring_e.step()
    ring_d[1].step()
    cross.wait_recv()

    def encode(i, _):
        rows = pl.ds(pl.multiple_of(384 * i, 384), 384)
        value = dot(res_all[i // 2, i % 2], enc_all[...].reshape(1024, 512)) + bias[...]
        pre[rows, :] = value
        active[rows, :] = jnp.maximum(value, 0.0).astype(BF16)
        return 0

    lax.fori_loop(0, 4, encode, 0)
    ring_d[0].step()

    def latent_rows(c, i):
        return pl.ds(pl.multiple_of(768 * c + 192 * i, 192), 192)

    def decode(t, c, i):
        return dot(active[latent_rows(c, i), :], dec_all[t].reshape(512, 1024)).reshape(4, 48, 1024)

    def hand(t, i):
        return remote(sent.at[t, i], crossed.at[t, i], psem.at[t, 0, i], psem.at[t, 1, i], other)

    def decode_other(t):
        def one(i, _):
            sent[t, i] = decode(t, 1 - core, i).astype(BF16)
            hand(t, i).start()
            return 0

        lax.fori_loop(0, 4, one, 0)

    def decode_mine(t):
        def one(i, _):
            value = decode(t, core, i)
            hand(t, i).wait_recv()
            mine[t, i] = (value + crossed[t, i].astype(F32)).astype(BF16)
            return 0

        lax.fori_loop(0, 4, one, 0)

    lo, hi = pl.ds(0, 512), pl.ds(512, 512)
    ok = valid[:, 0:1]

    def exchange(t):
        own, out = mine.at[t], grads.at[t, core]
        red_a = Reduce(
            4, x, east, west, lambda b: own.at[b, :, :, lo], lambda b, h: own.at[b, pl.ds(2 * h, 2), :, lo],
            [[a1.at[t, s], a2.at[t, s]] for s in range(2)], bsem.at[t, 0],
        )
        red_b = Reduce(
            4, y, north, south, lambda b: own.at[:, b, :, hi], lambda b, h: own.at[pl.ds(2 * h, 2), b, :, hi],
            [[b1.at[t, s], b2.at[t, s]] for s in range(2)], bsem.at[t, 1],
        )
        red_c = Reduce(
            4, y, north, south, lambda b: mid_a.at[t, b], lambda b, h: mid_a.at[t, b, :, pl.ds(256 * h, 256)],
            [[c1.at[t, s], c2.at[t, s]] for s in range(2)], bsem.at[t, 2],
        )
        red_d = Reduce(
            4, x, east, west, lambda b: mid_b.at[t, b], lambda b, h: mid_b.at[t, b, :, pl.ds(256 * h, 256)],
            [[d1.at[t, s], d2.at[t, s]] for s in range(2)], bsem.at[t, 3],
        )
        ring_c = Gather(
            4, y, north, south, lambda b: out.at[x, b, :, lo],
            lambda b, h: out.at[x, b, :, pl.ds(256 * h, 256)], bsem.at[t, 4],
        )
        ring_d = Gather(
            4, x, east, west, lambda b: out.at[b, y, :, hi],
            lambda b, h: out.at[b, y, :, pl.ds(512 + 256 * h, 256)], bsem.at[t, 5],
        )
        ring_a = Gather(
            4, x, east, west, lambda b: out.at[b, :, :, lo], lambda b, h: out.at[b, pl.ds(2 * h, 2), :, lo],
            bsem.at[t, 6],
        )
        ring_b = Gather(
            4, y, north, south, lambda b: out.at[:, b, :, hi], lambda b, h: out.at[pl.ds(2 * h, 2), b, :, hi],
            bsem.at[t, 7],
        )
        sum_y = Gather(4, y, north, south, lambda b: sq_y.at[b], None, sysem)
        sum_x = Gather(4, x, east, west, lambda b: sq_x.at[b], None, sxsem)
        sum_c = remote(sq_c.at[core], sq_c.at[core], scsem.at[0], scsem.at[1], other)
        cross = [remote(out.at[:, :, :, w], out.at[:, :, :, w], osem.at[t, i, 0], osem.at[t, i, 1], other)
                 for i, w in enumerate((lo, hi))]
        drains.extend([red_a, red_b, red_c, red_d, ring_a, ring_b, ring_c, ring_d])
        if t == 1:
            drains.extend([sum_y, sum_x])

        def misfit(where, landed, middle, at):
            rebuilt = middle[t, at].astype(F32) + landed[t, 0].astype(F32) + landed[t, 1].astype(F32)
            miss = (rebuilt - goal[t, :, where].astype(F32)) * ok
            out[x, y, :, where] = (scale * miss).astype(BF16)
            square = miss * miss
            parts = [square[8 * i : 8 * i + 8, 128 * j : 128 * j + 128] for i in range(6) for j in range(4)]
            squares[...] += sum(parts[1:], parts[0])

        red_a.step()
        red_b.step()
        yield
        red_a.step()
        red_b.step()
        yield
        red_a.step()
        mid_a[t] = (own[x, :, :, lo].astype(F32) + a2[t, 0].astype(F32) + a2[t, 1].astype(F32)).astype(BF16)
        red_c.step()
        red_b.step()
        mid_b[t] = (own[:, y, :, hi].astype(F32) + b2[t, 0].astype(F32) + b2[t, 1].astype(F32)).astype(BF16)
        red_d.step()
        yield
        red_c.step()
        red_d.step()
        yield
        red_c.step()
        misfit(lo, c2, mid_a, y)
        ring_c.step()
        red_d.step()
        misfit(hi, d2, mid_b, x)
        ring_d.step()
        if t == 1:
            sq_y[y] = squares[...]
            sum_y.step()
        yield
        ring_c.step()
        ring_d.step()
        if t == 1:
            sum_y.step()
        yield
        ring_c.step()
        ring_a.step()
        ring_d.step()
        ring_b.step()
        if t == 1:
            sum_y.step()
            sq_x[x] = (sq_y[0] + sq_y[1]) + (sq_y[2] + sq_y[3])
            sum_x.step()
        yield
        ring_a.step()
        ring_b.step()
        if t == 1:
            sum_x.step()
        yield
        ring_a.step()
        cross[0].start()
        ring_b.step()
        cross[1].start()
        if t == 1:
            sum_x.step()
            sq_c[core] = (sq_x[0] + sq_x[1]) + (sq_x[2] + sq_x[3])
            sum_c.start()
        yield
        cross[0].wait()
        cross[1].wait()
        if t == 1:
            sum_c.wait()
            small[z, :, 512:640] = sq_c[0] + sq_c[1]

    squares[...] = jnp.zeros_like(squares)
    first, second = exchange(0), exchange(1)

    def flip_features(i, _):
        res_t[:, cols(i, 384)] = res_all[i // 2, i % 2].T
        return 0

    def flip_latents(i, _):
        act_t[:, cols(i, 384)] = active[pl.ds(pl.multiple_of(384 * i, 384), 384), :].T
        return 0

    decode_other(0)
    decode_mine(0)
    next(first)
    ring_d[1].step()
    next(first)
    ring_d[1].step()
    next(first)
    lax.fori_loop(0, 4, flip_latents, 0)
    ring_d[1].step()
    decode_other(1)
    next(first)
    decode_mine(1)
    next(second)
    next(first)
    next(second)
    next(first)
    lax.fori_loop(0, 4, flip_features, 0)
    next(second)
    next(first)
    next(second)
    next(first)
    next(second)
    next(first)
    next(second)
    next(first, None)

    def decoder_product(t):
        def one(i, _):
            value = dot(act_t[...], grads[t, :, :, :, :, cols(i, 256)].reshape(1536, 256))
            dec_prod[t, :, :, cols(i, 256)] = value.astype(BF16).reshape(8, 64, 256)
            return 0

        lax.fori_loop(0, 4, one, 0)

    red_d = [
        Reduce(
            8, z, up, down, lambda b, t=t: dec_prod.at[t, b], lambda b, h, t=t: dec_prod.at[t, b, pl.ds(32 * h, 32)],
            [[dr1.at[t, s]] + [drn.at[t, s, i] for i in range(3)] for s in range(2)], dsem2.at[t],
        )
        for t in range(2)
    ]
    red_e = Reduce(
        8, z, up, down, lambda b: enc_prod.at[:, b], lambda b, h: enc_prod.at[h, b],
        [[er1.at[s]] + [ern.at[s, i] for i in range(3)] for s in range(2)], esem2,
    )
    ring_m = Gather(8, z, up, down, lambda b: small.at[b], None, msem)
    drains += red_d + [red_e, ring_m]
    next(second)
    decoder_product(0)
    red_d[0].step()

    def spread(t, c, i):
        return dot(grads[t, c, i].reshape(192, 1024), dec_all[t].reshape(512, 1024), ((1,), (1,)))

    def spread_first(i, _):
        back[latent_rows(i // 4, i % 4), :] = spread(0, i // 4, i % 4)
        return 0

    next(second)
    lax.fori_loop(0, 8, spread_first, 0)
    red_d[0].step()
    next(second)
    next(second, None)
    red_d[0].step()

    def spread_second(i, total):
        rows = latent_rows(i // 4, i % 4)
        value = back[rows, :] + spread(1, i // 4, i % 4)
        value = jnp.where(pre[rows, :] > 0, value, 0.0)
        narrow[rows, :] = value.astype(BF16)
        return total + jnp.sum(value.reshape(24, 8, 512), axis=0)

    total = lax.fori_loop(0, 8, spread_second, jnp.zeros((8, 512), F32))
    small[z, :, 0:512] = total
    ring_m.step()
    red_d[0].step()

    def encoder_product(i, _):
        rows = pl.ds(pl.multiple_of(256 * i, 256), 256)
        value = dot(res_t[rows, :], narrow[...])
        for j in range(4):
            enc_prod[i // 2, (i % 2) * 4 + j] = value[64 * j : 64 * j + 64].astype(BF16).reshape(2, 32, 512)
        return 0

    lax.fori_loop(0, 4, encoder_product, 0)
    red_e.step()
    decoder_product(1)
    red_d[1].step()
    red_d[0].step()
    ring_m.step()
    red_e.step()
    red_d[1].step()
    ring_m.step()
    red_e.step()
    red_d[1].step()
    ring_m.step()
    red_e.step()
    red_d[1].step()
    dec_out[0] = dec_prod[0, z].astype(F32) + drn[0, 0, 2].astype(F32) + drn[0, 1, 2].astype(F32)
    red_e.step()
    esum[...] = enc_prod[:, z].astype(F32) + ern[0, 2].astype(F32) + ern[1, 2].astype(F32)
    keep = [pltpu.make_async_copy(esum.at[x_hi, core], enc_out.at[x_hi, core], lsem.at[3])]
    keep[0].start()
    for i, (q, peer) in enumerate(zip(quad, quad_ids)):
        copy = remote(esum.at[q[0], q[1]], enc_out.at[x_hi, core], q2sem.at[0, i], q2sem.at[1, i], peer)
        copy.start()
        keep.append(copy)
    ring_m.step()
    full = ((small[0] + small[1]) + (small[2] + small[3])) + ((small[4] + small[5]) + (small[6] + small[7]))
    sq_out[...] = full[:, 512:640]
    small_sum[...] = full[:, 0:512]
    keep.append(pltpu.make_async_copy(small_sum, bias_out.at[x_hi, core], lsem.at[4]))
    keep[-1].start()
    for i, peer in enumerate(quad_ids):
        copy = remote(small_sum, bias_out.at[x_hi, core], q3sem.at[0, i], q3sem.at[1, i], peer)
        copy.start()
        keep.append(copy)
    red_d[1].step()
    dec_out[1] = dec_prod[1, z].astype(F32) + drn[1, 0, 2].astype(F32) + drn[1, 1, 2].astype(F32)
    for copy in keep:
        copy.wait()
    for copy in swap:
        copy.wait_send()
    cross.wait_send()
    for t in range(2):
        for i in range(4):
            hand(t, i).wait_send()
    for ring in drains:
        ring.drain()


VM = pl.BlockSpec(memory_space=pltpu.VMEM)


def dmas(*shape):
    return pltpu.SemaphoreType.DMA(shape)


def params(ident):
    return pltpu.CompilerParams(collective_id=ident, has_side_effects=True, vmem_limit_bytes=56 << 20)


def shape(*dims, dtype=BF16):
    return jax.ShapeDtypeStruct(dims, dtype)


def shards(residual, targets, counts, enc_weight, enc_bias, dec_weight):
    loop, dp = lax.axis_index("loop"), lax.axis_index("dp")
    x_hi, core = dp // 16, dp % 2
    enc_quad = enc_weight.reshape(32, 2, 8, 2, 64).transpose(1, 3, 0, 2, 4).reshape(2, 2, 32, 512)
    bias = lax.dynamic_index_in_dim(
        enc_bias.reshape(2, 8, 2, 64).transpose(0, 2, 1, 3).reshape(4, 512), x_hi * 2 + core, 0, True
    )
    goal = lax.dynamic_slice_in_dim(targets, loop * 48, 48, 0).transpose(1, 0, 2)
    rows = loop * 48 + lax.iota(jnp.int32, 48)
    valid = jnp.broadcast_to((rows < counts[0]).astype(F32)[:, None], (48, 128))
    total_rows = 32 * 384 // 2
    vm = pltpu.VMEM
    dec_grad, enc_grad, bias_grad, sq = pl.pallas_call(
        lambda *refs: step_kernel(2.0 / math.sqrt(total_rows), *refs),
        out_shape=(
            shape(2, 64, 1024, dtype=F32), shape(2, 2, 32, 512, dtype=F32),
            shape(2, 2, 8, 512, dtype=F32), shape(8, 128, dtype=F32),
        ),
        in_specs=[VM] * 6,
        out_specs=(VM,) * 4,
        scratch_shapes=[
            vm((2, 2, 384, 1024), BF16), vm((2, 8, 2, 32, 512), BF16), vm((2, 8, 64, 1024), BF16),
            vm((1536, 512), F32), vm((1536, 512), BF16), vm((512, 1536), BF16), vm((1024, 1536), BF16),
            vm((2, 4, 4, 48, 1024), BF16), vm((2, 4, 4, 48, 1024), BF16), vm((2, 4, 4, 48, 1024), BF16),
            vm((2, 2, 4, 4, 48, 1024), BF16),
            vm((2, 2, 2, 48, 512), BF16), vm((2, 2, 4, 48, 512), BF16),
            vm((2, 2, 2, 48, 512), BF16), vm((2, 2, 4, 48, 512), BF16),
            vm((2, 2, 48, 256), BF16), vm((2, 2, 48, 512), BF16),
            vm((2, 2, 48, 256), BF16), vm((2, 2, 48, 512), BF16),
            vm((2, 4, 48, 512), BF16), vm((2, 4, 48, 512), BF16),
            vm((1536, 512), F32), vm((1536, 512), BF16),
            vm((2, 8, 64, 1024), BF16), vm((2, 8, 2, 32, 512), BF16),
            vm((2, 2, 32, 1024), BF16), vm((2, 2, 3, 64, 1024), BF16),
            vm((2, 2, 32, 512), BF16), vm((2, 3, 2, 2, 32, 512), BF16), vm((2, 2, 32, 512), F32),
            vm((8, 128), F32), vm((4, 8, 128), F32), vm((4, 8, 128), F32), vm((2, 8, 128), F32),
            vm((8, 8, 640), F32), vm((8, 512), F32),
            dmas(2, 2, 2), dmas(2, 2, 2), dmas(2, 2, 4), dmas(2, 2, 2, 4), dmas(2, 3), dmas(2), dmas(5),
            dmas(2, 2, 4), dmas(2, 8, 2, 2, 2), dmas(2, 2, 2), dmas(2, 2, 2), dmas(2, 2, 2), dmas(2),
            dmas(2, 2, 2, 4), dmas(2, 2, 4), dmas(2, 2, 4), dmas(2, 3), dmas(2, 3),
        ],
        compiler_params=params(1),
    )(residual, enc_quad, dec_weight.transpose(1, 0, 2), bias, goal, valid)
    mean_error = jnp.sum(sq) / (total_rows * 2048)
    enc_grad = enc_grad.reshape(2, 2, 32, 8, 64).transpose(2, 0, 3, 1, 4).reshape(32, 2048)
    bias_grad = jnp.sum(bias_grad, axis=2).reshape(2, 2, 8, 64).transpose(0, 2, 1, 3).reshape(2048)
    return mean_error, enc_grad, bias_grad, dec_grad.transpose(1, 0, 2)


def solution(mesh):
    placed = (
        P("dp", "loop"),
        P("dp", None, None),
        P("dp"),
        P("dp", "loop"),
        P("loop"),
        P(("loop", "dp"), None, None),
    )
    return jax.shard_map(
        shards,
        mesh=mesh,
        in_specs=placed,
        out_specs=(P(), P("dp", "loop"), P("loop"), P(("loop", "dp"), None, None)),
        check_vma=False,
    )
```

```python
import math

import jax
import jax.numpy as jnp
from jax import lax
from jax.experimental import pallas as pl
from jax.experimental.pallas import tpu as pltpu
from jax.sharding import PartitionSpec as P

MESH = pl.DeviceIdType.MESH
BF16 = jnp.bfloat16
F32 = jnp.float32


def place():
    loop, dp = lax.axis_index("loop"), lax.axis_index("dp")
    x = (dp // 16) * 2 + loop // 4
    return x, loop % 4, (dp % 16) // 2, dp % 2


def ident(x, y, z, core):
    return ((x % 2) * 4 + y, (x // 2) * 16 + z * 2 + core)


def greet(peers):
    barrier = pltpu.get_barrier_semaphore()
    for peer in peers:
        pl.semaphore_signal(barrier, inc=1, device_id=peer, device_id_type=MESH)
    pl.semaphore_wait(barrier, len(peers))


def remote(src, dst, send, recv, peer):
    return pltpu.make_async_remote_copy(
        src_ref=src, dst_ref=dst, send_sem=send, recv_sem=recv, device_id=peer, device_id_type=MESH
    )


class Gather:
    def __init__(self, n, at, right, left, whole, half, sems):
        self.n, self.at, self.right, self.left = n, at, right, left
        self.whole, self.half, self.sems = whole, half, sems
        self.steps = []

    def step(self):
        s = len(self.steps)
        if s:
            for copy in self.steps[-1]:
                copy.wait_recv()
        if s == self.n // 2:
            return
        pair = []
        for side, peer in ((0, self.right), (1, self.left)):
            block = (self.at + (self.n - s if side == 0 else s)) % self.n
            last = s == self.n // 2 - 1
            if last and self.half is None and side == 1:
                continue
            ref = self.half(block, side) if last and self.half is not None else self.whole(block)
            copy = remote(ref, ref, self.sems.at[0, side, s], self.sems.at[1, side, s], peer)
            copy.start()
            pair.append(copy)
        self.steps.append(pair)

    def drain(self):
        for pair in self.steps:
            for copy in pair:
                copy.wait_send()


def add_into(ref, other):
    ref[...] = (ref[...].astype(F32) + other[...].astype(F32)).astype(BF16)


class Reduce:
    def __init__(self, n, at, right, left, whole, half, landed, sems):
        self.n, self.at, self.right, self.left = n, at, right, left
        self.whole, self.half, self.landed, self.sems = whole, half, landed, sems
        self.steps = []

    def step(self):
        s = len(self.steps)
        depth = self.n // 2
        pair = []
        for side, peer in ((0, self.right), (1, self.left)):
            if s:
                self.steps[-1][side].wait_recv()
            if s == depth:
                continue
            far = depth - s
            block = (self.at + (far if side == 0 else self.n - far)) % self.n
            if s:
                part = self.half(block, side) if s == 1 else self.whole(block)
                add_into(part, self.landed[side][s - 1])
            ref = self.half(block, side) if s == 0 else self.whole(block)
            copy = remote(ref, self.landed[side][s], self.sems.at[0, side, s], self.sems.at[1, side, s], peer)
            copy.start()
            pair.append(copy)
        if s < depth:
            self.steps.append(pair)

    def drain(self):
        for pair in self.steps:
            for copy in pair:
                copy.wait_send()


GROUPS = 4
ORDER = (
    "d31", "v1", "u1", "d01", "e1", "d21", "u2", "v2", "d02", "x1", "y1", "e2",
    "d32", "d11", "x2", "y2", "e3", "d03", "d33", "yw", "xw", "e4", "d12", "d04",
    "d22", "d34", "rw", "ew", "n0", "d13", "n1", "d0w", "o0", "f0", "d23", "d3w",
    "o3", "d14", "fl", "f3", "m0", "d24", "p000", "p010", "d1w", "o1", "m3", "p300",
    "d2w", "o2", "p310", "p001", "p011", "m1", "p100", "p110", "p301", "m2", "p210", "p200",
    "p311", "p002", "f1", "p012", "p101", "p211", "ff", "p013", "p312", "p201", "p003", "p302",
    "p111", "p212", "p014", "p102", "p313", "p004", "f2", "p303", "p202", "p213", "p015", "p314",
    "p103", "p005", "p112", "p203", "p304", "p016", "p315", "p214", "p113", "p006", "p305", "p204",
    "p104", "p316", "p114", "p215", "p306", "p205", "p017", "s1", "p105", "p007", "p115", "p216",
    "p206", "p317", "p307", "p018", "p008", "p116", "s2", "p106", "p217", "p019", "p207", "p009",
    "p318", "D0", "r01", "s3", "p308", "p107", "p319", "p117", "p218", "s4", "r02", "p309",
    "p208", "D3", "p108", "r31", "p118", "p209", "p219", "D2", "r21", "p109", "r03", "p119",
    "r32", "s5", "A", "s6", "r22", "r33", "B", "b1", "r23", "r04", "E0", "b2",
    "q01", "r24", "E1", "b3", "q11", "q02", "D1", "r11", "b4", "r2w", "q12", "q03",
    "r12", "r0w", "q13", "bw", "q04", "r13", "q14", "r34", "q0w", "r14", "q1w", "r3w",
    "r1w",
)


def dot(a, b, dims=((1,), (0,))):
    return lax.dot_general(a, b, (dims, ((), ())), preferred_element_type=F32)


def step_kernel(
    groups, scale, res, enc, dec, bias, goal, valid, dec_out, enc_out, bias_out, sq_out,
    res_all, enc_all, dec_all, pre, active, act_t, res_t, dec_t, sent, crossed, mine, grads,
    far1, far2, near1, near2, mid, back, narrow, dec_prod, enc_prod,
    dr1, drn, er1, ern, esum, squares, sq_y, sq_x, sq_c, small, small_sum,
    usem, vsem, ysem, xsem, esem, dsem, qsem, csem, lsem, psem, bsem, osem, sysem, sxsem, scsem,
    dsem2, esem2, msem, q2sem, q3sem,
):
    width = 2048 // groups
    wide, thin = width // 2, width // 4
    x, y, z, core = place()
    x_hi = x // 2
    up, down = ident(x, y, (z + 1) % 8, core), ident(x, y, (z + 7) % 8, core)
    east, west = ident((x + 1) % 4, y, z, core), ident((x + 3) % 4, y, z, core)
    north, south = ident(x, (y + 1) % 4, z, core), ident(x, (y + 3) % 4, z, core)
    other = ident(x, y, z, 1 - core)
    quad = [(1 - x_hi, core), (x_hi, 1 - core), (1 - x_hi, 1 - core)]
    quad_ids = [ident((x + 2) % 4, y, z, core), other, ident((x + 2) % 4, y, z, 1 - core)]
    drains = []

    def cols(block, width):
        return pl.ds(pl.multiple_of(block * width, width), width)

    top, low = pl.ds(0, 192), pl.ds(192, 192)

    def feature(rows, xx, yy):
        return res_all.at[core, xx // 2, rows, cols((xx % 2) * 4 + yy, 128)]

    def feature_row(rows, xx):
        return res_all.at[core, xx // 2, rows, cols(xx % 2, 512)]

    def feature_both(rows, k, yy):
        return res_all.at[core, :, rows, cols(k * 4 + yy, 128)]

    local = [
        pltpu.make_async_copy(res, feature(pl.ds(0, 384), x, y), lsem.at[0]),
        pltpu.make_async_copy(enc.at[x_hi, core], enc_all.at[x_hi, z, core], lsem.at[1]),
        pltpu.make_async_copy(dec, dec_all.at[:, z], lsem.at[2]),
    ]
    for copy in local:
        copy.start()
    greet([up, down, east, west, north, south] + quad_ids)
    swap = []
    for i, (q, peer) in enumerate(zip(quad, quad_ids)):
        copy = remote(enc.at[q[0], q[1]], enc_all.at[x_hi, z, core], qsem.at[0, i], qsem.at[1, i], peer)
        copy.start()
        swap.append(copy)
    for copy in local:
        copy.wait()
    ring_e = Gather(8, z, up, down, lambda b: enc_all.at[:, b], lambda b, h: enc_all.at[h, b], esem)
    ring_d = [
        Gather(
            8, z, up, down, lambda b, t=t: dec_all.at[t, b],
            lambda b, h, t=t: dec_all.at[t, b, pl.ds(32 * h, 32)], dsem.at[t],
        )
        for t in range(groups)
    ]
    ring_u = Gather(
        4, y, north, south, lambda b: feature(top, x, b), lambda b, h: feature(pl.ds(96 * h, 96), x, b), usem
    )
    ring_v = Gather(
        4, x, east, west, lambda b: feature(low, b, y), lambda b, h: feature(pl.ds(192 + 96 * h, 96), b, y), vsem
    )
    ring_x = Gather(
        4, x, east, west, lambda b: feature_row(top, b), lambda b, h: feature_row(pl.ds(96 * h, 96), b), xsem
    )
    ring_y = [
        Gather(
            4, y, north, south, lambda b, k=k: feature_both(low, k, b),
            lambda b, h, k=k: feature_both(pl.ds(192 + 96 * h, 96), k, b), ysem.at[k],
        )
        for k in range(2)
    ]
    drains += [ring_u, ring_v, ring_x, ring_e] + ring_y + ring_d

    tasks = {"e1": lambda: ([copy.wait_recv() for copy in swap], ring_e.step())}

    def put(*names):
        def bind(action):
            for name in names:
                tasks[name] = action
            return action

        return bind

    for name in ("e2", "e3", "e4", "ew"):
        tasks[name] = ring_e.step
    for g in range(groups):
        for name in "1234w":
            tasks[f"d{g}{name}"] = ring_d[g].step
    for name in ("u1", "u2"):
        tasks[name] = ring_u.step
    for name in ("v1", "v2"):
        tasks[name] = ring_v.step
    cross = []

    def cross_over(i, rows):
        ref = res_all.at[core, :, rows]
        cross.append(remote(ref, ref, csem.at[i, 0], csem.at[i, 1], other))
        cross[-1].start()

    tasks["x1"] = lambda: (ring_u.step(), ring_x.step())
    tasks["x2"] = ring_x.step
    tasks["xw"] = lambda: (ring_x.step(), cross_over(0, top))
    tasks["y1"] = lambda: (ring_v.step(), ring_y[0].step(), ring_y[1].step())
    tasks["y2"] = lambda: (ring_y[0].step(), ring_y[1].step())
    tasks["yw"] = lambda: (ring_y[0].step(), ring_y[1].step(), cross_over(1, low))
    tasks["rw"] = lambda: [copy.wait_recv() for copy in cross]

    def encode(i, _):
        rows = pl.ds(pl.multiple_of(384 * i, 384), 384)
        value = dot(res_all[i // 2, i % 2], enc_all[...].reshape(1024, 512)) + bias[...]
        pre[rows, :] = value
        active[rows, :] = jnp.maximum(value, 0.0).astype(BF16)
        return 0

    tasks["n0"] = lambda: lax.fori_loop(0, 2, encode, 0)
    tasks["n1"] = lambda: lax.fori_loop(2, 4, encode, 0)

    def flip_features(i, _):
        res_t[:, cols(i, 384)] = res_all[i // 2, i % 2].T
        return 0

    def flip_latents(i, _):
        act_t[:, cols(i, 384)] = active[pl.ds(pl.multiple_of(384 * i, 384), 384), :].T
        return 0

    def flip_decoder(g):
        def one(i, _):
            dec_t[g, :, cols(i, 128)] = dec_all[g, pl.ds(2 * i, 2)].reshape(128, width).T
            return 0

        lax.fori_loop(0, 4, one, 0)

    tasks["ff"] = lambda: lax.fori_loop(0, 4, flip_features, 0)
    tasks["fl"] = lambda: lax.fori_loop(0, 4, flip_latents, 0)

    def latent_rows(c, i):
        return pl.ds(pl.multiple_of(768 * c + 384 * i, 384), 384)

    def decode(g, c, i):
        return dot(active[latent_rows(c, i), :], dec_all[g].reshape(512, width)).reshape(2, 4, 48, width)

    def hand(g, i):
        pair = pl.ds(2 * i, 2)
        return remote(sent.at[g, pair], crossed.at[g, pair], psem.at[g, 0, i], psem.at[g, 1, i], other)

    def decode_other(g):
        def one(i, _):
            sent[g, pl.ds(2 * i, 2)] = decode(g, 1 - core, i).astype(BF16)
            hand(g, i).start()
            return 0

        lax.fori_loop(0, 2, one, 0)

    def decode_mine(g):
        def one(i, _):
            value = decode(g, core, i)
            hand(g, i).wait_recv()
            pair = pl.ds(2 * i, 2)
            mine[g, pair] = (value + crossed[g, pair].astype(F32)).astype(BF16)
            return 0

        lax.fori_loop(0, 2, one, 0)

    ok = valid[:, 0:1]
    along_x, along_y = (4, x, east, west), (4, y, north, south)
    squares[...] = jnp.zeros_like(squares)

    def exchange(g, q):
        own, out = mine.at[g], grads.at[g, core]
        w = pl.ds(q * wide, wide)
        first, then = (along_x, along_y) if q == 0 else (along_y, along_x)
        at, near = first[1], then[1]

        def lane(ref, b):
            return ref.at[b, :, :, w] if q == 0 else ref.at[:, b, :, w]

        def half_lane(ref, b, h):
            pair = pl.ds(2 * h, 2)
            return ref.at[b, pair, :, w] if q == 0 else ref.at[pair, b, :, w]

        def cell(b, where):
            return out.at[x, b, :, where] if q == 0 else out.at[b, y, :, where]

        def part(h):
            return pl.ds(q * wide + thin * h, thin)

        sems = bsem.at[g, q]
        red_far = Reduce(
            *first, lambda b: lane(own, b), lambda b, h: half_lane(own, b, h),
            [[far1.at[g, q, s], far2.at[g, q, s]] for s in range(2)], sems.at[0],
        )
        red_near = Reduce(
            *then, lambda b: mid.at[g, q, b], lambda b, h: mid.at[g, q, b, :, pl.ds(thin * h, thin)],
            [[near1.at[g, q, s], near2.at[g, q, s]] for s in range(2)], sems.at[1],
        )
        ring_near = Gather(*then, lambda b: cell(b, w), lambda b, h: cell(b, part(h)), sems.at[2])
        ring_far = Gather(*first, lambda b: lane(out, b), lambda b, h: half_lane(out, b, h), sems.at[3])
        drains.extend([red_far, red_near, ring_near, ring_far])
        over = []

        def hand_over(k):
            ref = lane(out, (at + k) % 4)
            over.append(remote(ref, ref, osem.at[g, q, 0, k], osem.at[g, q, 1, k], other))
            over[-1].start()

        red_far.step()
        yield
        red_far.step()
        yield
        red_far.step()
        mid[g, q] = (
            lane(own, at)[...].astype(F32) + far2[g, q, 0].astype(F32) + far2[g, q, 1].astype(F32)
        ).astype(BF16)
        red_near.step()
        yield
        red_near.step()
        yield
        red_near.step()
        rebuilt = mid[g, q, near].astype(F32) + near2[g, q, 0].astype(F32) + near2[g, q, 1].astype(F32)
        miss = (rebuilt - goal[g, :, w].astype(F32)) * ok
        cell(near, w)[...] = (scale * miss).astype(BF16)
        ring_near.step()
        square = miss * miss
        parts = [
            square[8 * i : 8 * i + 8, 128 * j : 128 * j + 128] for i in range(6) for j in range(wide // 128)
        ]
        squares[...] += sum(parts[1:], parts[0])
        yield
        ring_near.step()
        yield
        ring_near.step()
        ring_far.step()
        hand_over(0)
        yield
        ring_far.step()
        hand_over(1)
        hand_over(3)
        yield
        ring_far.step()
        hand_over(2)
        yield
        for copy in over:
            copy.wait()
        yield

    def decoder_product(g):
        def one(i, _):
            value = dot(act_t[...], grads[g, :, :, :, :, cols(i, 256)].reshape(1536, 256))
            dec_prod[g, :, :, cols(i, 256)] = value.astype(BF16).reshape(8, 64, 256)
            return 0

        lax.fori_loop(0, width // 256, one, 0)

    def finish_decoder(g, ring):
        ring.step()
        dec_out[g] = dec_prod[g, z].astype(F32) + drn[g, 0, 2].astype(F32) + drn[g, 1, 2].astype(F32)

    for g in range(groups):
        tasks[f"o{g}"] = lambda g=g: decode_other(g)
        tasks[f"m{g}"] = lambda g=g: decode_mine(g)
        tasks[f"f{g}"] = lambda g=g: flip_decoder(g)
        for q in range(2):
            flow = exchange(g, q)
            for k in range(10):
                tasks[f"p{g}{q}{k}"] = lambda flow=flow: next(flow)
        ring = Reduce(
            8, z, up, down, lambda b, g=g: dec_prod.at[g, b],
            lambda b, h, g=g: dec_prod.at[g, b, pl.ds(32 * h, 32)],
            [[dr1.at[g, s]] + [drn.at[g, s, i] for i in range(3)] for s in range(2)], dsem2.at[g],
        )
        drains.append(ring)
        tasks[f"D{g}"] = lambda g=g: decoder_product(g)
        for k in range(1, 5):
            tasks[f"r{g}{k}"] = ring.step
        tasks[f"r{g}w"] = lambda g=g, ring=ring: finish_decoder(g, ring)

    sum_y = Gather(*along_y, lambda b: sq_y.at[b], None, sysem)
    sum_x = Gather(*along_x, lambda b: sq_x.at[b], None, sxsem)
    sum_c = remote(sq_c.at[core], sq_c.at[core], scsem.at[0], scsem.at[1], other)
    drains += [sum_y, sum_x]
    tasks["s2"] = sum_y.step
    tasks["s4"] = sum_x.step

    @put("s1")
    def _():
        sq_y[y] = squares[...]
        sum_y.step()

    @put("s3")
    def _():
        sum_y.step()
        sq_x[x] = (sq_y[0] + sq_y[1]) + (sq_y[2] + sq_y[3])
        sum_x.step()

    @put("s5")
    def _():
        sum_x.step()
        sq_c[core] = (sq_x[0] + sq_x[1]) + (sq_x[2] + sq_x[3])
        sum_c.start()

    @put("s6")
    def _():
        sum_c.wait()
        small[z, :, 512:640] = sq_c[0] + sq_c[1]

    def spread(some, c, i):
        terms = [dot(grads[g, c, pl.ds(2 * i, 2)].reshape(384, width), dec_t[g]) for g in some]
        return sum(terms[1:], terms[0])

    def spread_first(i, _):
        back[latent_rows(i // 2, i % 2), :] = spread(range(groups - 1), i // 2, i % 2)
        return 0

    def spread_last(i, total):
        rows = latent_rows(i // 2, i % 2)
        value = back[rows, :] + spread((groups - 1,), i // 2, i % 2)
        value = jnp.where(pre[rows, :] > 0, value, 0.0)
        narrow[rows, :] = value.astype(BF16)
        return total + jnp.sum(value.reshape(48, 8, 512), axis=0)

    tasks["A"] = lambda: lax.fori_loop(0, 4, spread_first, 0)

    @put("B")
    def _():
        small[z, :, 0:512] = lax.fori_loop(0, 4, spread_last, jnp.zeros((8, 512), F32))

    ring_m = Gather(8, z, up, down, lambda b: small.at[b], None, msem)
    drains.append(ring_m)
    for k in range(1, 5):
        tasks[f"b{k}"] = ring_m.step
    keep = []

    @put("bw")
    def _():
        ring_m.step()
        full = ((small[0] + small[1]) + (small[2] + small[3])) + ((small[4] + small[5]) + (small[6] + small[7]))
        sq_out[...] = full[:, 512:640]
        small_sum[...] = full[:, 0:512]
        keep.append(pltpu.make_async_copy(small_sum, bias_out.at[x_hi, core], lsem.at[4]))
        keep[-1].start()
        for i, peer in enumerate(quad_ids):
            copy = remote(small_sum, bias_out.at[x_hi, core], q3sem.at[0, i], q3sem.at[1, i], peer)
            copy.start()
            keep.append(copy)

    def encoder_product(i, side):
        value = dot(res_t[pl.ds(pl.multiple_of(512 * side, 512), 512), :], narrow[...])
        enc_prod[side] = value.astype(BF16).reshape(8, 2, 32, 512)

    def finish_encoder(i, side, ring):
        ring.step()
        esum[side] = enc_prod[side, z].astype(F32) + ern[i, 0, 2].astype(F32) + ern[i, 1, 2].astype(F32)
        for j, (q, peer) in enumerate(zip(quad, quad_ids)):
            if (j == 1) == (i == 1):
                copy = remote(esum.at[q[0], q[1]], enc_out.at[x_hi, core], q2sem.at[0, j], q2sem.at[1, j], peer)
                copy.start()
                keep.append(copy)
        if i == 1:
            keep.append(pltpu.make_async_copy(esum.at[x_hi, core], enc_out.at[x_hi, core], lsem.at[3]))
            keep[-1].start()

    for i, side in enumerate((1 - x_hi, x_hi)):
        ring = Reduce(
            8, z, up, down, lambda b, side=side: enc_prod.at[side, b],
            lambda b, h, side=side: enc_prod.at[side, b, h],
            [[er1.at[i, s]] + [ern.at[i, s, k] for k in range(3)] for s in range(2)], esem2.at[i],
        )
        drains.append(ring)
        tasks[f"E{i}"] = lambda i=i, side=side: encoder_product(i, side)
        for k in range(1, 5):
            tasks[f"q{i}{k}"] = ring.step
        tasks[f"q{i}w"] = lambda i=i, side=side, ring=ring: finish_encoder(i, side, ring)

    for name in ORDER:
        tasks[name]()
    for copy in keep:
        copy.wait()
    for copy in swap + cross:
        copy.wait_send()
    for g in range(groups):
        for i in range(2):
            hand(g, i).wait_send()
    for ring in drains:
        ring.drain()


VM = pl.BlockSpec(memory_space=pltpu.VMEM)


def dmas(*shape):
    return pltpu.SemaphoreType.DMA(shape)


def params(ident):
    return pltpu.CompilerParams(collective_id=ident, has_side_effects=True, vmem_limit_bytes=56 << 20)


def shape(*dims, dtype=BF16):
    return jax.ShapeDtypeStruct(dims, dtype)


def shards(residual, targets, counts, enc_weight, enc_bias, dec_weight):
    loop, dp = lax.axis_index("loop"), lax.axis_index("dp")
    x_hi, core = dp // 16, dp % 2
    enc_quad = enc_weight.reshape(32, 2, 8, 2, 64).transpose(1, 3, 0, 2, 4).reshape(2, 2, 32, 512)
    bias = lax.dynamic_index_in_dim(
        enc_bias.reshape(2, 8, 2, 64).transpose(0, 2, 1, 3).reshape(4, 512), x_hi * 2 + core, 0, True
    )
    n = GROUPS
    width = 2048 // n
    wide, thin = width // 2, width // 4
    goal = lax.dynamic_slice_in_dim(targets, loop * 48, 48, 0).reshape(48, n, width).transpose(1, 0, 2)
    rows = loop * 48 + lax.iota(jnp.int32, 48)
    valid = jnp.broadcast_to((rows < counts[0]).astype(F32)[:, None], (48, 128))
    total_rows = 32 * 384 // 2
    vm = pltpu.VMEM
    dec_grad, enc_grad, bias_grad, sq = pl.pallas_call(
        lambda *refs: step_kernel(n, 2.0 / math.sqrt(total_rows), *refs),
        out_shape=(
            shape(n, 64, width, dtype=F32), shape(2, 2, 32, 512, dtype=F32),
            shape(2, 2, 8, 512, dtype=F32), shape(8, 128, dtype=F32),
        ),
        in_specs=[pl.BlockSpec(memory_space=pl.ANY)] * 3 + [VM] * 3,
        out_specs=(VM,) * 4,
        scratch_shapes=[
            vm((2, 2, 384, 1024), BF16), vm((2, 8, 2, 32, 512), BF16), vm((n, 8, 64, width), BF16),
            vm((1536, 512), F32), vm((1536, 512), BF16), vm((512, 1536), BF16), vm((1024, 1536), BF16),
            vm((n, width, 512), BF16),
            vm((n, 4, 4, 48, width), BF16), vm((n, 4, 4, 48, width), BF16), vm((n, 4, 4, 48, width), BF16),
            vm((n, 2, 4, 4, 48, width), BF16),
            vm((n, 2, 2, 2, 48, wide), BF16), vm((n, 2, 2, 4, 48, wide), BF16),
            vm((n, 2, 2, 48, thin), BF16), vm((n, 2, 2, 48, wide), BF16), vm((n, 2, 4, 48, wide), BF16),
            vm((1536, 512), F32), vm((1536, 512), BF16),
            vm((n, 8, 64, width), BF16), vm((2, 8, 2, 32, 512), BF16),
            vm((n, 2, 32, width), BF16), vm((n, 2, 3, 64, width), BF16),
            vm((2, 2, 32, 512), BF16), vm((2, 2, 3, 2, 32, 512), BF16), vm((2, 2, 32, 512), F32),
            vm((8, 128), F32), vm((4, 8, 128), F32), vm((4, 8, 128), F32), vm((2, 8, 128), F32),
            vm((8, 8, 640), F32), vm((8, 512), F32),
            dmas(2, 2, 2), dmas(2, 2, 2), dmas(2, 2, 2, 2), dmas(2, 2, 2), dmas(2, 2, 4), dmas(n, 2, 2, 4),
            dmas(2, 3), dmas(2, 2), dmas(5), dmas(n, 2, 2), dmas(n, 2, 4, 2, 2, 2), dmas(n, 2, 2, 4),
            dmas(2, 2, 2), dmas(2, 2, 2), dmas(2), dmas(n, 2, 2, 4), dmas(2, 2, 2, 4), dmas(2, 2, 4),
            dmas(2, 3), dmas(2, 3),
        ],
        compiler_params=params(1),
    )(residual, enc_quad, dec_weight.reshape(64, n, width).transpose(1, 0, 2), bias, goal, valid)
    mean_error = jnp.sum(sq) / (total_rows * 2048)
    enc_grad = enc_grad.reshape(2, 2, 32, 8, 64).transpose(2, 0, 3, 1, 4).reshape(32, 2048)
    bias_grad = jnp.sum(bias_grad, axis=2).reshape(2, 2, 8, 64).transpose(0, 2, 1, 3).reshape(2048)
    return mean_error, enc_grad, bias_grad, dec_grad.transpose(1, 0, 2).reshape(64, 2, 1024)


def solution(mesh):
    placed = (
        P("dp", "loop"),
        P("dp", None, None),
        P("dp"),
        P("dp", "loop"),
        P("loop"),
        P(("loop", "dp"), None, None),
    )
    return jax.shard_map(
        shards,
        mesh=mesh,
        in_specs=placed,
        out_specs=(P(), P("dp", "loop"), P("loop"), P(("loop", "dp"), None, None)),
        check_vma=False,
    )
```

```python
import math

import jax
import jax.numpy as jnp
from jax import lax
from jax.experimental import pallas as pl
from jax.experimental.pallas import tpu as pltpu
from jax.sharding import PartitionSpec as P

MESH = pl.DeviceIdType.MESH
BF16 = jnp.bfloat16
F32 = jnp.float32


def place():
    loop, dp = lax.axis_index("loop"), lax.axis_index("dp")
    x = (dp // 16) * 2 + loop // 4
    return x, loop % 4, (dp % 16) // 2, dp % 2


def ident(x, y, z, core):
    return ((x % 2) * 4 + y, (x // 2) * 16 + z * 2 + core)


def greet(peers):
    barrier = pltpu.get_barrier_semaphore()
    for peer in peers:
        pl.semaphore_signal(barrier, inc=1, device_id=peer, device_id_type=MESH)
    pl.semaphore_wait(barrier, len(peers))


def remote(src, dst, send, recv, peer):
    return pltpu.make_async_remote_copy(
        src_ref=src, dst_ref=dst, send_sem=send, recv_sem=recv, device_id=peer, device_id_type=MESH
    )


class Gather:
    def __init__(self, n, at, right, left, whole, half, sems):
        self.n, self.at, self.right, self.left = n, at, right, left
        self.whole, self.half, self.sems = whole, half, sems
        self.steps = []

    def step(self):
        s = len(self.steps)
        if s:
            for copy in self.steps[-1]:
                copy.wait_recv()
        if s == self.n // 2:
            return
        pair = []
        for side, peer in ((0, self.right), (1, self.left)):
            block = (self.at + (self.n - s if side == 0 else s)) % self.n
            last = s == self.n // 2 - 1
            if last and self.half is None and side == 1:
                continue
            ref = self.half(block, side) if last and self.half is not None else self.whole(block)
            copy = remote(ref, ref, self.sems.at[0, side, s], self.sems.at[1, side, s], peer)
            copy.start()
            pair.append(copy)
        self.steps.append(pair)

    def drain(self):
        for pair in self.steps:
            for copy in pair:
                copy.wait_send()


def add_into(ref, other):
    ref[...] = (ref[...].astype(F32) + other[...].astype(F32)).astype(BF16)


class Reduce:
    def __init__(self, n, at, right, left, whole, half, landed, sems):
        self.n, self.at, self.right, self.left = n, at, right, left
        self.whole, self.half, self.landed, self.sems = whole, half, landed, sems
        self.steps = []

    def step(self):
        s = len(self.steps)
        depth = self.n // 2
        pair = []
        for side, peer in ((0, self.right), (1, self.left)):
            if s:
                self.steps[-1][side].wait_recv()
            if s == depth:
                continue
            far = depth - s
            block = (self.at + (far if side == 0 else self.n - far)) % self.n
            if s:
                part = self.half(block, side) if s == 1 else self.whole(block)
                add_into(part, self.landed[side][s - 1])
            ref = self.half(block, side) if s == 0 else self.whole(block)
            copy = remote(ref, self.landed[side][s], self.sems.at[0, side, s], self.sems.at[1, side, s], peer)
            copy.start()
            pair.append(copy)
        if s < depth:
            self.steps.append(pair)

    def drain(self):
        for pair in self.steps:
            for copy in pair:
                copy.wait_send()


GROUPS = 4
ORDER = (
    "d31", "v1", "u1", "d01", "e1", "d21", "u2", "v2", "d02", "x1", "y1", "e2",
    "d32", "d11", "x2", "y2", "e3", "d03", "d33", "yw", "xw", "e4", "d12", "d04",
    "d22", "d34", "rw", "ew", "n0", "d13", "n1", "d0w", "o0", "f0", "d23", "d3w",
    "o3", "d14", "fl", "f3", "m0", "d24", "p000", "p010", "d1w", "o1", "m3", "p300",
    "d2w", "o2", "p310", "p001", "p011", "m1", "p100", "p110", "p301", "m2", "p210", "p200",
    "p311", "p002", "f1", "p012", "p101", "p211", "ff", "p013", "p312", "p201", "p003", "p302",
    "p111", "p212", "p014", "p102", "p313", "p004", "f2", "p303", "p202", "p213", "p015", "p314",
    "p103", "p005", "p112", "p203", "p304", "p016", "p315", "p214", "p113", "p006", "p305", "p204",
    "p104", "p316", "p114", "p215", "p306", "p205", "p017", "s1", "p105", "p007", "p115", "p216",
    "p206", "p317", "p307", "p018", "p008", "p116", "s2", "p106", "p217", "p019", "p207", "p009",
    "p318", "D0", "r01", "s3", "p308", "p107", "p319", "p117", "p218", "s4", "r02", "p309",
    "p208", "D3", "p108", "r31", "p118", "p209", "p219", "D2", "r21", "p109", "r03", "p119",
    "r32", "s5", "A", "s6", "r22", "r33", "B", "b1", "r23", "r04", "E0", "b2",
    "q01", "r24", "E1", "b3", "q11", "q02", "D1", "r11", "b4", "r2w", "q12", "q03",
    "r12", "r0w", "q13", "bw", "q04", "r13", "q14", "r34", "q0w", "r14", "q1w", "r3w",
    "r1w",
)


def dot(a, b, dims=((1,), (0,))):
    return lax.dot_general(a, b, (dims, ((), ())), preferred_element_type=F32)


def step_kernel(
    groups, total_rows, counts, res, enc_in, dec, bias_in, goal, dec_out, enc_grad, bias_grad, loss,
    enc, bias, enc_out, bias_out, res_all, enc_all, dec_all, pre, active, act_t, res_t, dec_t, sent, crossed, mine, grads,
    far1, far2, near1, near2, mid, back, narrow, dec_prod, enc_prod,
    dr1, drn, er1, ern, esum, squares, sq_y, sq_x, sq_c, small, small_sum,
    usem, vsem, ysem, xsem, esem, dsem, qsem, csem, lsem, psem, bsem, osem, sysem, sxsem, scsem,
    dsem2, esem2, msem, q2sem, q3sem,
):
    width = 2048 // groups
    wide, thin = width // 2, width // 4
    scale = 2.0 / math.sqrt(total_rows)
    x, y, z, core = place()
    x_hi = x // 2
    up, down = ident(x, y, (z + 1) % 8, core), ident(x, y, (z + 7) % 8, core)
    east, west = ident((x + 1) % 4, y, z, core), ident((x + 3) % 4, y, z, core)
    north, south = ident(x, (y + 1) % 4, z, core), ident(x, (y + 3) % 4, z, core)
    other = ident(x, y, z, 1 - core)
    quad = [(1 - x_hi, core), (x_hi, 1 - core), (1 - x_hi, 1 - core)]
    quad_ids = [ident((x + 2) % 4, y, z, core), other, ident((x + 2) % 4, y, z, 1 - core)]
    drains = []

    def cols(block, width):
        return pl.ds(pl.multiple_of(block * width, width), width)

    top, low = pl.ds(0, 192), pl.ds(192, 192)

    def feature(rows, xx, yy):
        return res_all.at[core, xx // 2, rows, cols((xx % 2) * 4 + yy, 128)]

    def feature_row(rows, xx):
        return res_all.at[core, xx // 2, rows, cols(xx % 2, 512)]

    def feature_both(rows, k, yy):
        return res_all.at[core, :, rows, cols(k * 4 + yy, 128)]

    def column(g):
        return divmod(g * width, 1024)

    local = [pltpu.make_async_copy(res, feature(pl.ds(0, 384), x, y), lsem.at[0])]
    for g in range(groups):
        t, at = column(g)
        local.append(pltpu.make_async_copy(dec.at[t, :, pl.ds(at, width)], dec_all.at[g, z], lsem.at[2 + g]))
    for copy in local:
        copy.start()
    runs = [(h, c, k, 1024 * h + 128 * k + 64 * c) for h in range(2) for c in range(2) for k in range(8)]
    for h, c, k, at in runs:
        enc[h, c, :, 64 * k : 64 * k + 64] = enc_in[:, at : at + 64]
    local.append(pltpu.make_async_copy(enc.at[x_hi, core], enc_all.at[x_hi, z, core], lsem.at[1]))
    local[-1].start()
    both = bias_in[pl.ds(pl.multiple_of(8 * x_hi, 8), 8), :]
    chosen = jnp.where(core == 0, both[:, 0:64], both[:, 64:128])
    for k in range(8):
        bias[:, 64 * k : 64 * k + 64] = chosen[k : k + 1, :]
    greet([up, down, east, west, north, south] + quad_ids)
    swap = []
    for i, (q, peer) in enumerate(zip(quad, quad_ids)):
        copy = remote(enc.at[q[0], q[1]], enc_all.at[x_hi, z, core], qsem.at[0, i], qsem.at[1, i], peer)
        copy.start()
        swap.append(copy)
    for copy in local:
        copy.wait()
    ring_e = Gather(8, z, up, down, lambda b: enc_all.at[:, b], lambda b, h: enc_all.at[h, b], esem)
    ring_d = [
        Gather(
            8, z, up, down, lambda b, t=t: dec_all.at[t, b],
            lambda b, h, t=t: dec_all.at[t, b, pl.ds(32 * h, 32)], dsem.at[t],
        )
        for t in range(groups)
    ]
    ring_u = Gather(
        4, y, north, south, lambda b: feature(top, x, b), lambda b, h: feature(pl.ds(96 * h, 96), x, b), usem
    )
    ring_v = Gather(
        4, x, east, west, lambda b: feature(low, b, y), lambda b, h: feature(pl.ds(192 + 96 * h, 96), b, y), vsem
    )
    ring_x = Gather(
        4, x, east, west, lambda b: feature_row(top, b), lambda b, h: feature_row(pl.ds(96 * h, 96), b), xsem
    )
    ring_y = [
        Gather(
            4, y, north, south, lambda b, k=k: feature_both(low, k, b),
            lambda b, h, k=k: feature_both(pl.ds(192 + 96 * h, 96), k, b), ysem.at[k],
        )
        for k in range(2)
    ]
    drains += [ring_u, ring_v, ring_x, ring_e] + ring_y + ring_d

    tasks = {"e1": lambda: ([copy.wait_recv() for copy in swap], ring_e.step())}

    def put(*names):
        def bind(action):
            for name in names:
                tasks[name] = action
            return action

        return bind

    for name in ("e2", "e3", "e4", "ew"):
        tasks[name] = ring_e.step
    for g in range(groups):
        for name in "1234w":
            tasks[f"d{g}{name}"] = ring_d[g].step
    for name in ("u1", "u2"):
        tasks[name] = ring_u.step
    for name in ("v1", "v2"):
        tasks[name] = ring_v.step
    cross = []

    def cross_over(i, rows):
        ref = res_all.at[core, :, rows]
        cross.append(remote(ref, ref, csem.at[i, 0], csem.at[i, 1], other))
        cross[-1].start()

    tasks["x1"] = lambda: (ring_u.step(), ring_x.step())
    tasks["x2"] = ring_x.step
    tasks["xw"] = lambda: (ring_x.step(), cross_over(0, top))
    tasks["y1"] = lambda: (ring_v.step(), ring_y[0].step(), ring_y[1].step())
    tasks["y2"] = lambda: (ring_y[0].step(), ring_y[1].step())
    tasks["yw"] = lambda: (ring_y[0].step(), ring_y[1].step(), cross_over(1, low))
    tasks["rw"] = lambda: [copy.wait_recv() for copy in cross]

    def encode(i, _):
        rows = pl.ds(pl.multiple_of(384 * i, 384), 384)
        value = dot(res_all[i // 2, i % 2], enc_all[...].reshape(1024, 512)) + bias[...]
        pre[rows, :] = value
        active[rows, :] = jnp.maximum(value, 0.0).astype(BF16)
        return 0

    tasks["n0"] = lambda: lax.fori_loop(0, 2, encode, 0)
    tasks["n1"] = lambda: lax.fori_loop(2, 4, encode, 0)

    def flip_features(i, _):
        res_t[:, cols(i, 384)] = res_all[i // 2, i % 2].T
        return 0

    def flip_latents(i, _):
        act_t[:, cols(i, 384)] = active[pl.ds(pl.multiple_of(384 * i, 384), 384), :].T
        return 0

    def flip_decoder(g):
        def one(i, _):
            dec_t[g, :, cols(i, 128)] = dec_all[g, pl.ds(2 * i, 2)].reshape(128, width).T
            return 0

        lax.fori_loop(0, 4, one, 0)

    tasks["ff"] = lambda: lax.fori_loop(0, 4, flip_features, 0)
    tasks["fl"] = lambda: lax.fori_loop(0, 4, flip_latents, 0)

    def latent_rows(c, i):
        return pl.ds(pl.multiple_of(768 * c + 384 * i, 384), 384)

    def decode(g, c, i):
        return dot(active[latent_rows(c, i), :], dec_all[g].reshape(512, width)).reshape(2, 4, 48, width)

    def hand(g, i):
        pair = pl.ds(2 * i, 2)
        return remote(sent.at[g, pair], crossed.at[g, pair], psem.at[g, 0, i], psem.at[g, 1, i], other)

    def decode_other(g):
        def one(i, _):
            sent[g, pl.ds(2 * i, 2)] = decode(g, 1 - core, i).astype(BF16)
            hand(g, i).start()
            return 0

        lax.fori_loop(0, 2, one, 0)

    def decode_mine(g):
        def one(i, _):
            value = decode(g, core, i)
            hand(g, i).wait_recv()
            pair = pl.ds(2 * i, 2)
            mine[g, pair] = (value + crossed[g, pair].astype(F32)).astype(BF16)
            return 0

        lax.fori_loop(0, 2, one, 0)

    row = ((x % 2) * 4 + y) * 48 + lax.broadcasted_iota(jnp.int32, (48, 128), 0)
    ok = (row < counts[0]).astype(F32)[:, 0:1]
    along_x, along_y = (4, x, east, west), (4, y, north, south)
    squares[...] = jnp.zeros_like(squares)

    def exchange(g, q):
        own, out = mine.at[g], grads.at[g, core]
        t, start = column(g)
        w = pl.ds(q * wide, wide)
        first, then = (along_x, along_y) if q == 0 else (along_y, along_x)
        at, near = first[1], then[1]

        def lane(ref, b):
            return ref.at[b, :, :, w] if q == 0 else ref.at[:, b, :, w]

        def half_lane(ref, b, h):
            pair = pl.ds(2 * h, 2)
            return ref.at[b, pair, :, w] if q == 0 else ref.at[pair, b, :, w]

        def cell(b, where):
            return out.at[x, b, :, where] if q == 0 else out.at[b, y, :, where]

        def part(h):
            return pl.ds(q * wide + thin * h, thin)

        sems = bsem.at[g, q]
        red_far = Reduce(
            *first, lambda b: lane(own, b), lambda b, h: half_lane(own, b, h),
            [[far1.at[g, q, s], far2.at[g, q, s]] for s in range(2)], sems.at[0],
        )
        red_near = Reduce(
            *then, lambda b: mid.at[g, q, b], lambda b, h: mid.at[g, q, b, :, pl.ds(thin * h, thin)],
            [[near1.at[g, q, s], near2.at[g, q, s]] for s in range(2)], sems.at[1],
        )
        ring_near = Gather(*then, lambda b: cell(b, w), lambda b, h: cell(b, part(h)), sems.at[2])
        ring_far = Gather(*first, lambda b: lane(out, b), lambda b, h: half_lane(out, b, h), sems.at[3])
        drains.extend([red_far, red_near, ring_near, ring_far])
        over = []

        def hand_over(k):
            ref = lane(out, (at + k) % 4)
            over.append(remote(ref, ref, osem.at[g, q, 0, k], osem.at[g, q, 1, k], other))
            over[-1].start()

        red_far.step()
        yield
        red_far.step()
        yield
        red_far.step()
        mid[g, q] = (
            lane(own, at)[...].astype(F32) + far2[g, q, 0].astype(F32) + far2[g, q, 1].astype(F32)
        ).astype(BF16)
        red_near.step()
        yield
        red_near.step()
        yield
        red_near.step()
        rebuilt = mid[g, q, near].astype(F32) + near2[g, q, 0].astype(F32) + near2[g, q, 1].astype(F32)
        miss = (rebuilt - goal[t, :, pl.ds(start + q * wide, wide)].astype(F32)) * ok
        cell(near, w)[...] = (scale * miss).astype(BF16)
        ring_near.step()
        square = miss * miss
        parts = [
            square[8 * i : 8 * i + 8, 128 * j : 128 * j + 128] for i in range(6) for j in range(wide // 128)
        ]
        squares[...] += sum(parts[1:], parts[0])
        yield
        ring_near.step()
        yield
        ring_near.step()
        ring_far.step()
        hand_over(0)
        yield
        ring_far.step()
        hand_over(1)
        hand_over(3)
        yield
        ring_far.step()
        hand_over(2)
        yield
        for copy in over:
            copy.wait()
        yield

    def decoder_product(g):
        def one(i, _):
            value = dot(act_t[...], grads[g, :, :, :, :, cols(i, 256)].reshape(1536, 256))
            dec_prod[g, :, :, cols(i, 256)] = value.astype(BF16).reshape(8, 64, 256)
            return 0

        lax.fori_loop(0, width // 256, one, 0)

    def finish_decoder(g, ring):
        ring.step()
        t, at = column(g)
        dec_out[t, :, at : at + width] = dec_prod[g, z].astype(F32) + drn[g, 0, 2].astype(F32) + drn[g, 1, 2].astype(F32)

    for g in range(groups):
        tasks[f"o{g}"] = lambda g=g: decode_other(g)
        tasks[f"m{g}"] = lambda g=g: decode_mine(g)
        tasks[f"f{g}"] = lambda g=g: flip_decoder(g)
        for q in range(2):
            flow = exchange(g, q)
            for k in range(10):
                tasks[f"p{g}{q}{k}"] = lambda flow=flow: next(flow)
        ring = Reduce(
            8, z, up, down, lambda b, g=g: dec_prod.at[g, b],
            lambda b, h, g=g: dec_prod.at[g, b, pl.ds(32 * h, 32)],
            [[dr1.at[g, s]] + [drn.at[g, s, i] for i in range(3)] for s in range(2)], dsem2.at[g],
        )
        drains.append(ring)
        tasks[f"D{g}"] = lambda g=g: decoder_product(g)
        for k in range(1, 5):
            tasks[f"r{g}{k}"] = ring.step
        tasks[f"r{g}w"] = lambda g=g, ring=ring: finish_decoder(g, ring)

    sum_y = Gather(*along_y, lambda b: sq_y.at[b], None, sysem)
    sum_x = Gather(*along_x, lambda b: sq_x.at[b], None, sxsem)
    sum_c = remote(sq_c.at[core], sq_c.at[core], scsem.at[0], scsem.at[1], other)
    drains += [sum_y, sum_x]
    tasks["s2"] = sum_y.step
    tasks["s4"] = sum_x.step

    @put("s1")
    def _():
        sq_y[y] = squares[...]
        sum_y.step()

    @put("s3")
    def _():
        sum_y.step()
        sq_x[x] = (sq_y[0] + sq_y[1]) + (sq_y[2] + sq_y[3])
        sum_x.step()

    @put("s5")
    def _():
        sum_x.step()
        sq_c[core] = (sq_x[0] + sq_x[1]) + (sq_x[2] + sq_x[3])
        sum_c.start()

    @put("s6")
    def _():
        sum_c.wait()
        small[z, :, 512:640] = sq_c[0] + sq_c[1]

    def spread(some, c, i):
        terms = [dot(grads[g, c, pl.ds(2 * i, 2)].reshape(384, width), dec_t[g]) for g in some]
        return sum(terms[1:], terms[0])

    def spread_first(i, _):
        back[latent_rows(i // 2, i % 2), :] = spread(range(groups - 1), i // 2, i % 2)
        return 0

    def spread_last(i, total):
        rows = latent_rows(i // 2, i % 2)
        value = back[rows, :] + spread((groups - 1,), i // 2, i % 2)
        value = jnp.where(pre[rows, :] > 0, value, 0.0)
        narrow[rows, :] = value.astype(BF16)
        return total + jnp.sum(value.reshape(48, 8, 512), axis=0)

    tasks["A"] = lambda: lax.fori_loop(0, 4, spread_first, 0)

    @put("B")
    def _():
        small[z, :, 0:512] = lax.fori_loop(0, 4, spread_last, jnp.zeros((8, 512), F32))

    ring_m = Gather(8, z, up, down, lambda b: small.at[b], None, msem)
    drains.append(ring_m)
    for k in range(1, 5):
        tasks[f"b{k}"] = ring_m.step
    keep = []

    @put("bw")
    def _():
        ring_m.step()
        full = ((small[0] + small[1]) + (small[2] + small[3])) + ((small[4] + small[5]) + (small[6] + small[7]))
        loss[0] = jnp.sum(full[:, 512:640]) / (total_rows * 2048)
        small_sum[...] = full[:, 0:512]
        keep.append(pltpu.make_async_copy(small_sum, bias_out.at[x_hi, core], lsem.at[2 + groups]))
        keep[-1].start()
        for i, peer in enumerate(quad_ids):
            copy = remote(small_sum, bias_out.at[x_hi, core], q3sem.at[0, i], q3sem.at[1, i], peer)
            copy.start()
            keep.append(copy)

    def encoder_product(i, side):
        value = dot(res_t[pl.ds(pl.multiple_of(512 * side, 512), 512), :], narrow[...])
        enc_prod[side] = value.astype(BF16).reshape(8, 2, 32, 512)

    def finish_encoder(i, side, ring):
        ring.step()
        esum[side] = enc_prod[side, z].astype(F32) + ern[i, 0, 2].astype(F32) + ern[i, 1, 2].astype(F32)
        for j, (q, peer) in enumerate(zip(quad, quad_ids)):
            if (j == 1) == (i == 1):
                copy = remote(esum.at[q[0], q[1]], enc_out.at[x_hi, core], q2sem.at[0, j], q2sem.at[1, j], peer)
                copy.start()
                keep.append(copy)
        if i == 1:
            keep.append(pltpu.make_async_copy(esum.at[x_hi, core], enc_out.at[x_hi, core], lsem.at[3 + groups]))
            keep[-1].start()

    for i, side in enumerate((1 - x_hi, x_hi)):
        ring = Reduce(
            8, z, up, down, lambda b, side=side: enc_prod.at[side, b],
            lambda b, h, side=side: enc_prod.at[side, b, h],
            [[er1.at[i, s]] + [ern.at[i, s, k] for k in range(3)] for s in range(2)], esem2.at[i],
        )
        drains.append(ring)
        tasks[f"E{i}"] = lambda i=i, side=side: encoder_product(i, side)
        for k in range(1, 5):
            tasks[f"q{i}{k}"] = ring.step
        tasks[f"q{i}w"] = lambda i=i, side=side, ring=ring: finish_encoder(i, side, ring)

    for name in ORDER:
        tasks[name]()
    for copy in keep:
        copy.wait()
    sums = [[jnp.sum(bias_out[h, c], axis=0, keepdims=True) for c in range(2)] for h in range(2)]
    for h, c, k, at in runs:
        enc_grad[:, at : at + 64] = enc_out[h, c, :, 64 * k : 64 * k + 64]
        bias_grad[8 * h + k : 8 * h + k + 1, 64 * c : 64 * c + 64] = sums[h][c][:, 64 * k : 64 * k + 64]
    for copy in swap + cross:
        copy.wait_send()
    for g in range(groups):
        for i in range(2):
            hand(g, i).wait_send()
    for ring in drains:
        ring.drain()


VM = pl.BlockSpec(memory_space=pltpu.VMEM)


def dmas(*shape):
    return pltpu.SemaphoreType.DMA(shape)


def params(ident):
    return pltpu.CompilerParams(collective_id=ident, has_side_effects=True, vmem_limit_bytes=56 << 20)


def shape(*dims, dtype=BF16):
    return jax.ShapeDtypeStruct(dims, dtype)


SM = pl.BlockSpec(memory_space=pltpu.SMEM)


def shards(residual, targets, counts, enc_weight, enc_bias, dec_weight):
    n = GROUPS
    width = 2048 // n
    wide, thin = width // 2, width // 4
    goal = lax.dynamic_slice_in_dim(targets, lax.axis_index("loop") * 48, 48, 0).transpose(1, 0, 2)
    total_rows = 32 * 384 // 2
    vm = pltpu.VMEM
    dec_grad, enc_grad, bias_grad, loss = pl.pallas_call(
        lambda *refs: step_kernel(n, total_rows, *refs),
        out_shape=(
            shape(2, 64, 1024, dtype=F32), shape(32, 2048, dtype=F32), shape(16, 128, dtype=F32), shape(1, dtype=F32),
        ),
        in_specs=[SM, pl.BlockSpec(memory_space=pl.ANY), VM, pl.BlockSpec(memory_space=pl.ANY), VM, VM],
        out_specs=(VM, VM, VM, SM),
        scratch_shapes=[
            vm((2, 2, 32, 512), BF16), vm((1, 512), F32), vm((2, 2, 32, 512), F32), vm((2, 2, 8, 512), F32),
            vm((2, 2, 384, 1024), BF16), vm((2, 8, 2, 32, 512), BF16), vm((n, 8, 64, width), BF16),
            vm((1536, 512), F32), vm((1536, 512), BF16), vm((512, 1536), BF16), vm((1024, 1536), BF16),
            vm((n, width, 512), BF16),
            vm((n, 4, 4, 48, width), BF16), vm((n, 4, 4, 48, width), BF16), vm((n, 4, 4, 48, width), BF16),
            vm((n, 2, 4, 4, 48, width), BF16),
            vm((n, 2, 2, 2, 48, wide), BF16), vm((n, 2, 2, 4, 48, wide), BF16),
            vm((n, 2, 2, 48, thin), BF16), vm((n, 2, 2, 48, wide), BF16), vm((n, 2, 4, 48, wide), BF16),
            vm((1536, 512), F32), vm((1536, 512), BF16),
            vm((n, 8, 64, width), BF16), vm((2, 8, 2, 32, 512), BF16),
            vm((n, 2, 32, width), BF16), vm((n, 2, 3, 64, width), BF16),
            vm((2, 2, 32, 512), BF16), vm((2, 2, 3, 2, 32, 512), BF16), vm((2, 2, 32, 512), F32),
            vm((8, 128), F32), vm((4, 8, 128), F32), vm((4, 8, 128), F32), vm((2, 8, 128), F32),
            vm((8, 8, 640), F32), vm((8, 512), F32),
            dmas(2, 2, 2), dmas(2, 2, 2), dmas(2, 2, 2, 2), dmas(2, 2, 2), dmas(2, 2, 4), dmas(n, 2, 2, 4),
            dmas(2, 3), dmas(2, 2), dmas(n + 4), dmas(n, 2, 2), dmas(n, 2, 4, 2, 2, 2), dmas(n, 2, 2, 4),
            dmas(2, 2, 2), dmas(2, 2, 2), dmas(2), dmas(n, 2, 2, 4), dmas(2, 2, 2, 4), dmas(2, 2, 4),
            dmas(2, 3), dmas(2, 3),
        ],
        compiler_params=params(1),
    )(counts, residual, enc_weight, dec_weight.transpose(1, 0, 2), enc_bias.reshape(16, 128), goal)
    return loss.reshape(()), enc_grad, bias_grad.reshape(2048), dec_grad.transpose(1, 0, 2)


def solution(mesh):
    placed = (
        P("dp", "loop"),
        P("dp", None, None),
        P("dp"),
        P("dp", "loop"),
        P("loop"),
        P(("loop", "dp"), None, None),
    )
    return jax.shard_map(
        shards,
        mesh=mesh,
        in_specs=placed,
        out_specs=(P(), P("dp", "loop"), P("loop"), P(("loop", "dp"), None, None)),
        check_vma=False,
    )
```

```python
import math

import jax
import jax.numpy as jnp
from jax import lax
from jax.experimental import pallas as pl
from jax.experimental.pallas import tpu as pltpu
from jax.sharding import PartitionSpec as P

MESH = pl.DeviceIdType.MESH
BF16 = jnp.bfloat16
F32 = jnp.float32


def place():
    loop, dp = lax.axis_index("loop"), lax.axis_index("dp")
    x = (dp // 16) * 2 + loop // 4
    return x, loop % 4, (dp % 16) // 2, dp % 2


def ident(x, y, z, core):
    return ((x % 2) * 4 + y, (x // 2) * 16 + z * 2 + core)


def greet(peers):
    barrier = pltpu.get_barrier_semaphore()
    for peer in peers:
        pl.semaphore_signal(barrier, inc=1, device_id=peer, device_id_type=MESH)
    pl.semaphore_wait(barrier, len(peers))


def remote(src, dst, send, recv, peer):
    return pltpu.make_async_remote_copy(
        src_ref=src, dst_ref=dst, send_sem=send, recv_sem=recv, device_id=peer, device_id_type=MESH
    )


class Gather:
    def __init__(self, n, at, right, left, whole, half, sems):
        self.n, self.at, self.right, self.left = n, at, right, left
        self.whole, self.half, self.sems = whole, half, sems
        self.steps = []

    def step(self):
        s = len(self.steps)
        if s:
            for copy in self.steps[-1]:
                copy.wait_recv()
        if s == self.n // 2:
            return
        pair = []
        for side, peer in ((0, self.right), (1, self.left)):
            block = (self.at + (self.n - s if side == 0 else s)) % self.n
            last = s == self.n // 2 - 1
            if last and self.half is None and side == 1:
                continue
            ref = self.half(block, side) if last and self.half is not None else self.whole(block)
            copy = remote(ref, ref, self.sems.at[0, side, s], self.sems.at[1, side, s], peer)
            copy.start()
            pair.append(copy)
        self.steps.append(pair)

    def drain(self):
        for pair in self.steps:
            for copy in pair:
                copy.wait_send()


def add_into(ref, other):
    ref[...] = (ref[...].astype(F32) + other[...].astype(F32)).astype(BF16)


class Reduce:
    def __init__(self, n, at, right, left, whole, half, landed, sems):
        self.n, self.at, self.right, self.left = n, at, right, left
        self.whole, self.half, self.landed, self.sems = whole, half, landed, sems
        self.steps = []

    def step(self):
        s = len(self.steps)
        depth = self.n // 2
        pair = []
        for side, peer in ((0, self.right), (1, self.left)):
            if s:
                self.steps[-1][side].wait_recv()
            if s == depth:
                continue
            far = depth - s
            block = (self.at + (far if side == 0 else self.n - far)) % self.n
            if s:
                part = self.half(block, side) if s == 1 else self.whole(block)
                add_into(part, self.landed[side][s - 1])
            ref = self.half(block, side) if s == 0 else self.whole(block)
            copy = remote(ref, self.landed[side][s], self.sems.at[0, side, s], self.sems.at[1, side, s], peer)
            copy.start()
            pair.append(copy)
        if s < depth:
            self.steps.append(pair)

    def drain(self):
        for pair in self.steps:
            for copy in pair:
                copy.wait_send()


GROUPS = 4
ORDER = (
    "d01", "v1", "u1", "e1", "d11", "v2", "u2", "d02", "e2", "y1", "x1", "d21",
    "d12", "e3", "x2", "d03", "d31", "y2", "e4", "d13", "d22", "xw", "d04", "d32",
    "yw", "ew", "n0", "d14", "rw", "n1", "d23", "d0w", "o0", "d33", "f0", "d1w",
    "o1", "d24", "m0", "p010", "p000", "d34", "m1", "d2w", "o2", "p110", "p100", "p011",
    "d3w", "p001", "o3", "m2", "p200", "p210", "p101", "p111", "m3", "p012", "p002", "p300",
    "p310", "p201", "p211", "ff", "p102", "p013", "p003", "p112", "p301", "p311", "f1", "fl",
    "f3", "p212", "p202", "p103", "p014", "p113", "p004", "f2", "p302", "p312", "p203", "p213",
    "p104", "p015", "p114", "p005", "p303", "p313", "p204", "p214", "p105", "p016", "p115", "p006",
    "p304", "p314", "s1", "p205", "p215", "p116", "p106", "p017", "s2", "p007", "p315", "p305",
    "p216", "p206", "p117", "p107", "p018", "p008", "p316", "p306", "p019", "s3", "p009", "p217",
    "p207", "p118", "D0", "p108", "p119", "r01", "p317", "p307", "p109", "p218", "D1", "p208",
    "p219", "r11", "r02", "p318", "p209", "D2", "p308", "r21", "p319", "s4", "r12", "p309",
    "D3", "r31", "r03", "r22", "A", "r13", "s5", "r32", "B", "s6", "b1", "r23",
    "E0", "q01", "r04", "E1", "q11", "b2", "q02", "r33", "q12", "b3", "q03", "r24",
    "q13", "r0w", "q04", "b4", "r2w", "r14", "q14", "q0w", "r34", "bw", "q1w", "r1w",
    "r3w",
)


def dot(a, b, dims=((1,), (0,))):
    return lax.dot_general(a, b, (dims, ((), ())), preferred_element_type=F32)


def step_kernel(
    groups, total_rows, counts, res, enc_in, dec, bias_in, goal, dec_out, enc_grad, bias_grad, loss,
    enc, bias, enc_out, bias_out, res_all, enc_all, dec_all, pre, active, act_t, res_t, dec_t, sent, crossed, mine, grads,
    far1, far2, near1, near2, mid, back, narrow, dec_prod, enc_prod,
    dr1, drn, er1, ern, esum, squares, sq_y, sq_x, sq_c, small, small_sum,
    usem, vsem, ysem, xsem, esem, dsem, qsem, csem, lsem, psem, bsem, osem, sysem, sxsem, scsem,
    dsem2, esem2, msem, q2sem, q3sem,
):
    width = 2048 // groups
    wide, thin = width // 2, width // 4
    scale = 2.0 / math.sqrt(total_rows)
    x, y, z, core = place()
    x_hi = x // 2
    up, down = ident(x, y, (z + 1) % 8, core), ident(x, y, (z + 7) % 8, core)
    east, west = ident((x + 1) % 4, y, z, core), ident((x + 3) % 4, y, z, core)
    north, south = ident(x, (y + 1) % 4, z, core), ident(x, (y + 3) % 4, z, core)
    other = ident(x, y, z, 1 - core)
    quad = [(1 - x_hi, core), (x_hi, 1 - core), (1 - x_hi, 1 - core)]
    quad_ids = [ident((x + 2) % 4, y, z, core), other, ident((x + 2) % 4, y, z, 1 - core)]
    drains = []

    def cols(block, width):
        return pl.ds(pl.multiple_of(block * width, width), width)

    top, low = pl.ds(0, 192), pl.ds(192, 192)

    def feature(rows, xx, yy):
        return res_all.at[core, xx // 2, rows, cols((xx % 2) * 4 + yy, 128)]

    def feature_row(rows, xx):
        return res_all.at[core, xx // 2, rows, cols(xx % 2, 512)]

    def feature_both(rows, k, yy):
        return res_all.at[core, :, rows, cols(k * 4 + yy, 128)]

    def column(g):
        return divmod(g * width, 1024)

    local = [pltpu.make_async_copy(res, feature(pl.ds(0, 384), x, y), lsem.at[0])]
    for g in range(groups):
        t, at = column(g)
        local.append(pltpu.make_async_copy(dec.at[t, :, pl.ds(at, width)], dec_all.at[g, z], lsem.at[2 + g]))
    for copy in local:
        copy.start()
    runs = [(h, c, k, 1024 * h + 128 * k + 64 * c) for h in range(2) for c in range(2) for k in range(8)]
    for h, c, k, at in runs:
        enc[h, c, :, 64 * k : 64 * k + 64] = enc_in[:, at : at + 64]
    local.append(pltpu.make_async_copy(enc.at[x_hi, core], enc_all.at[x_hi, z, core], lsem.at[1]))
    local[-1].start()
    both = bias_in[pl.ds(pl.multiple_of(8 * x_hi, 8), 8), :]
    chosen = jnp.where(core == 0, both[:, 0:64], both[:, 64:128])
    for k in range(8):
        bias[:, 64 * k : 64 * k + 64] = chosen[k : k + 1, :]
    greet([up, down, east, west, north, south] + quad_ids)
    swap = []
    for i, (q, peer) in enumerate(zip(quad, quad_ids)):
        copy = remote(enc.at[q[0], q[1]], enc_all.at[x_hi, z, core], qsem.at[0, i], qsem.at[1, i], peer)
        copy.start()
        swap.append(copy)
    for copy in local:
        copy.wait()
    ring_e = Gather(8, z, up, down, lambda b: enc_all.at[:, b], lambda b, h: enc_all.at[h, b], esem)
    ring_d = [
        Gather(
            8, z, up, down, lambda b, t=t: dec_all.at[t, b],
            lambda b, h, t=t: dec_all.at[t, b, pl.ds(32 * h, 32)], dsem.at[t],
        )
        for t in range(groups)
    ]
    ring_u = Gather(
        4, y, north, south, lambda b: feature(top, x, b), lambda b, h: feature(pl.ds(96 * h, 96), x, b), usem
    )
    ring_v = Gather(
        4, x, east, west, lambda b: feature(low, b, y), lambda b, h: feature(pl.ds(192 + 96 * h, 96), b, y), vsem
    )
    ring_x = Gather(
        4, x, east, west, lambda b: feature_row(top, b), lambda b, h: feature_row(pl.ds(96 * h, 96), b), xsem
    )
    ring_y = [
        Gather(
            4, y, north, south, lambda b, k=k: feature_both(low, k, b),
            lambda b, h, k=k: feature_both(pl.ds(192 + 96 * h, 96), k, b), ysem.at[k],
        )
        for k in range(2)
    ]
    drains += [ring_u, ring_v, ring_x, ring_e] + ring_y + ring_d

    tasks = {"e1": lambda: ([copy.wait_recv() for copy in swap], ring_e.step())}

    def put(*names):
        def bind(action):
            for name in names:
                tasks[name] = action
            return action

        return bind

    for name in ("e2", "e3", "e4", "ew"):
        tasks[name] = ring_e.step
    for g in range(groups):
        for name in "1234w":
            tasks[f"d{g}{name}"] = ring_d[g].step
    for name in ("u1", "u2"):
        tasks[name] = ring_u.step
    for name in ("v1", "v2"):
        tasks[name] = ring_v.step
    cross = []

    def cross_over(i, rows):
        ref = res_all.at[core, :, rows]
        cross.append(remote(ref, ref, csem.at[i, 0], csem.at[i, 1], other))
        cross[-1].start()

    tasks["x1"] = lambda: (ring_u.step(), ring_x.step())
    tasks["x2"] = ring_x.step
    tasks["xw"] = lambda: (ring_x.step(), cross_over(0, top))
    tasks["y1"] = lambda: (ring_v.step(), ring_y[0].step(), ring_y[1].step())
    tasks["y2"] = lambda: (ring_y[0].step(), ring_y[1].step())
    tasks["yw"] = lambda: (ring_y[0].step(), ring_y[1].step(), cross_over(1, low))
    tasks["rw"] = lambda: [copy.wait_recv() for copy in cross]

    def encode(k, _):
        i = (2 * core + k) % 4
        rows = pl.ds(pl.multiple_of(384 * i, 384), 384)
        value = dot(res_all[i // 2, i % 2], enc_all[...].reshape(1024, 512)) + bias[...]
        pre[rows, :] = value
        active[rows, :] = jnp.maximum(value, 0.0).astype(BF16)
        return 0

    tasks["n0"] = lambda: lax.fori_loop(0, 2, encode, 0)
    tasks["n1"] = lambda: lax.fori_loop(2, 4, encode, 0)

    def flip_features(i, _):
        res_t[:, cols(i, 384)] = res_all[i // 2, i % 2].T
        return 0

    def flip_latents(i, _):
        act_t[:, cols(i, 384)] = active[pl.ds(pl.multiple_of(384 * i, 384), 384), :].T
        return 0

    def flip_decoder(g):
        def one(i, _):
            dec_t[g, :, cols(i, 128)] = dec_all[g, pl.ds(2 * i, 2)].reshape(128, width).T
            return 0

        lax.fori_loop(0, 4, one, 0)

    tasks["ff"] = lambda: lax.fori_loop(0, 4, flip_features, 0)
    tasks["fl"] = lambda: lax.fori_loop(0, 4, flip_latents, 0)

    def latent_rows(c, i):
        return pl.ds(pl.multiple_of(768 * c + 384 * i, 384), 384)

    def decode(g, c, i):
        return dot(active[latent_rows(c, i), :], dec_all[g].reshape(512, width)).reshape(2, 4, 48, width)

    def hand(g, i):
        pair = pl.ds(2 * i, 2)
        return remote(sent.at[g, pair], crossed.at[g, pair], psem.at[g, 0, i], psem.at[g, 1, i], other)

    def decode_other(g):
        def one(i, _):
            sent[g, pl.ds(2 * i, 2)] = decode(g, 1 - core, i).astype(BF16)
            hand(g, i).start()
            return 0

        lax.fori_loop(0, 2, one, 0)

    def decode_mine(g):
        def one(i, _):
            value = decode(g, core, i)
            hand(g, i).wait_recv()
            pair = pl.ds(2 * i, 2)
            mine[g, pair] = (value + crossed[g, pair].astype(F32)).astype(BF16)
            return 0

        lax.fori_loop(0, 2, one, 0)

    row = ((x % 2) * 4 + y) * 48 + lax.broadcasted_iota(jnp.int32, (48, 128), 0)
    ok = (row < counts[0]).astype(F32)[:, 0:1]
    along_x, along_y = (4, x, east, west), (4, y, north, south)
    squares[...] = jnp.zeros_like(squares)

    def exchange(g, q):
        own, out = mine.at[g], grads.at[g, core]
        t, start = column(g)
        w = pl.ds(q * wide, wide)
        first, then = (along_x, along_y) if q == 0 else (along_y, along_x)
        at, near = first[1], then[1]

        def lane(ref, b):
            return ref.at[b, :, :, w] if q == 0 else ref.at[:, b, :, w]

        def half_lane(ref, b, h):
            pair = pl.ds(2 * h, 2)
            return ref.at[b, pair, :, w] if q == 0 else ref.at[pair, b, :, w]

        def cell(b, where):
            return out.at[x, b, :, where] if q == 0 else out.at[b, y, :, where]

        def part(h):
            return pl.ds(q * wide + thin * h, thin)

        sems = bsem.at[g, q]
        red_far = Reduce(
            *first, lambda b: lane(own, b), lambda b, h: half_lane(own, b, h),
            [[far1.at[g, q, s], far2.at[g, q, s]] for s in range(2)], sems.at[0],
        )
        red_near = Reduce(
            *then, lambda b: mid.at[g, q, b], lambda b, h: mid.at[g, q, b, :, pl.ds(thin * h, thin)],
            [[near1.at[g, q, s], near2.at[g, q, s]] for s in range(2)], sems.at[1],
        )
        ring_near = Gather(*then, lambda b: cell(b, w), lambda b, h: cell(b, part(h)), sems.at[2])
        ring_far = Gather(*first, lambda b: lane(out, b), lambda b, h: half_lane(out, b, h), sems.at[3])
        drains.extend([red_far, red_near, ring_near, ring_far])
        over = []

        def hand_over(k):
            ref = lane(out, (at + k) % 4)
            over.append(remote(ref, ref, osem.at[g, q, 0, k], osem.at[g, q, 1, k], other))
            over[-1].start()

        red_far.step()
        yield
        red_far.step()
        yield
        red_far.step()
        mid[g, q] = (
            lane(own, at)[...].astype(F32) + far2[g, q, 0].astype(F32) + far2[g, q, 1].astype(F32)
        ).astype(BF16)
        red_near.step()
        yield
        red_near.step()
        yield
        red_near.step()
        rebuilt = mid[g, q, near].astype(F32) + near2[g, q, 0].astype(F32) + near2[g, q, 1].astype(F32)
        miss = (rebuilt - goal[t, :, pl.ds(start + q * wide, wide)].astype(F32)) * ok
        cell(near, w)[...] = (scale * miss).astype(BF16)
        ring_near.step()
        square = miss * miss
        parts = [
            square[8 * i : 8 * i + 8, 128 * j : 128 * j + 128] for i in range(6) for j in range(wide // 128)
        ]
        squares[...] += sum(parts[1:], parts[0])
        yield
        ring_near.step()
        yield
        ring_near.step()
        ring_far.step()
        hand_over(0)
        yield
        ring_far.step()
        hand_over(1)
        hand_over(3)
        yield
        ring_far.step()
        hand_over(2)
        yield
        for copy in over:
            copy.wait()
        yield

    def decoder_product(g):
        value = dot(act_t[...], grads[g].reshape(1536, width))
        dec_prod[g] = value.astype(BF16).reshape(8, 64, width)

    def finish_decoder(g, ring):
        ring.step()
        t, at = column(g)
        dec_out[t, :, at : at + width] = dec_prod[g, z].astype(F32) + drn[g, 0, 2].astype(F32) + drn[g, 1, 2].astype(F32)

    for g in range(groups):
        tasks[f"o{g}"] = lambda g=g: decode_other(g)
        tasks[f"m{g}"] = lambda g=g: decode_mine(g)
        tasks[f"f{g}"] = lambda g=g: flip_decoder(g)
        for q in range(2):
            flow = exchange(g, q)
            for k in range(10):
                tasks[f"p{g}{q}{k}"] = lambda flow=flow: next(flow)
        ring = Reduce(
            8, z, up, down, lambda b, g=g: dec_prod.at[g, b],
            lambda b, h, g=g: dec_prod.at[g, b, pl.ds(32 * h, 32)],
            [[dr1.at[g, s]] + [drn.at[g, s, i] for i in range(3)] for s in range(2)], dsem2.at[g],
        )
        drains.append(ring)
        tasks[f"D{g}"] = lambda g=g: decoder_product(g)
        for k in range(1, 5):
            tasks[f"r{g}{k}"] = ring.step
        tasks[f"r{g}w"] = lambda g=g, ring=ring: finish_decoder(g, ring)

    sum_y = Gather(*along_y, lambda b: sq_y.at[b], None, sysem)
    sum_x = Gather(*along_x, lambda b: sq_x.at[b], None, sxsem)
    sum_c = remote(sq_c.at[core], sq_c.at[core], scsem.at[0], scsem.at[1], other)
    drains += [sum_y, sum_x]
    tasks["s2"] = sum_y.step
    tasks["s4"] = sum_x.step

    @put("s1")
    def _():
        sq_y[y] = squares[...]
        sum_y.step()

    @put("s3")
    def _():
        sum_y.step()
        sq_x[x] = (sq_y[0] + sq_y[1]) + (sq_y[2] + sq_y[3])
        sum_x.step()

    @put("s5")
    def _():
        sum_x.step()
        sq_c[core] = (sq_x[0] + sq_x[1]) + (sq_x[2] + sq_x[3])
        sum_c.start()

    @put("s6")
    def _():
        sum_c.wait()
        small[z, :, 512:640] = sq_c[0] + sq_c[1]

    def spread(some, c, i):
        terms = [dot(grads[g, c, pl.ds(2 * i, 2)].reshape(384, width), dec_t[g]) for g in some]
        return sum(terms[1:], terms[0])

    def spread_first(i, _):
        back[latent_rows(i // 2, i % 2), :] = spread(range(groups - 1), i // 2, i % 2)
        return 0

    def spread_last(i, total):
        rows = latent_rows(i // 2, i % 2)
        value = back[rows, :] + spread((groups - 1,), i // 2, i % 2)
        value = jnp.where(pre[rows, :] > 0, value, 0.0)
        narrow[rows, :] = value.astype(BF16)
        return total + jnp.sum(value.reshape(48, 8, 512), axis=0)

    tasks["A"] = lambda: lax.fori_loop(0, 4, spread_first, 0)

    @put("B")
    def _():
        small[z, :, 0:512] = lax.fori_loop(0, 4, spread_last, jnp.zeros((8, 512), F32))

    ring_m = Gather(8, z, up, down, lambda b: small.at[b], None, msem)
    drains.append(ring_m)
    for k in range(1, 5):
        tasks[f"b{k}"] = ring_m.step
    keep = []

    @put("bw")
    def _():
        ring_m.step()
        full = ((small[0] + small[1]) + (small[2] + small[3])) + ((small[4] + small[5]) + (small[6] + small[7]))
        loss[0] = jnp.sum(full[:, 512:640]) / (total_rows * 2048)
        small_sum[...] = full[:, 0:512]
        keep.append(pltpu.make_async_copy(small_sum, bias_out.at[x_hi, core], lsem.at[2 + groups]))
        keep[-1].start()
        for i, peer in enumerate(quad_ids):
            copy = remote(small_sum, bias_out.at[x_hi, core], q3sem.at[0, i], q3sem.at[1, i], peer)
            copy.start()
            keep.append(copy)

    def encoder_product(i, side):
        value = dot(res_t[pl.ds(pl.multiple_of(512 * side, 512), 512), :], narrow[...])
        enc_prod[side] = value.astype(BF16).reshape(8, 2, 32, 512)

    def finish_encoder(i, side, ring):
        ring.step()
        esum[side] = enc_prod[side, z].astype(F32) + ern[i, 0, 2].astype(F32) + ern[i, 1, 2].astype(F32)
        for j, (q, peer) in enumerate(zip(quad, quad_ids)):
            if (j == 1) == (i == 1):
                copy = remote(esum.at[q[0], q[1]], enc_out.at[x_hi, core], q2sem.at[0, j], q2sem.at[1, j], peer)
                copy.start()
                keep.append(copy)
        if i == 1:
            keep.append(pltpu.make_async_copy(esum.at[x_hi, core], enc_out.at[x_hi, core], lsem.at[3 + groups]))
            keep[-1].start()

    for i, side in enumerate((1 - x_hi, x_hi)):
        ring = Reduce(
            8, z, up, down, lambda b, side=side: enc_prod.at[side, b],
            lambda b, h, side=side: enc_prod.at[side, b, h],
            [[er1.at[i, s]] + [ern.at[i, s, k] for k in range(3)] for s in range(2)], esem2.at[i],
        )
        drains.append(ring)
        tasks[f"E{i}"] = lambda i=i, side=side: encoder_product(i, side)
        for k in range(1, 5):
            tasks[f"q{i}{k}"] = ring.step
        tasks[f"q{i}w"] = lambda i=i, side=side, ring=ring: finish_encoder(i, side, ring)

    for name in ORDER:
        tasks[name]()
    for copy in keep:
        copy.wait()
    sums = [[jnp.sum(bias_out[h, c], axis=0, keepdims=True) for c in range(2)] for h in range(2)]
    for h, c, k, at in runs:
        enc_grad[:, at : at + 64] = enc_out[h, c, :, 64 * k : 64 * k + 64]
        bias_grad[8 * h + k : 8 * h + k + 1, 64 * c : 64 * c + 64] = sums[h][c][:, 64 * k : 64 * k + 64]
    for copy in swap + cross:
        copy.wait_send()
    for g in range(groups):
        for i in range(2):
            hand(g, i).wait_send()
    for ring in drains:
        ring.drain()


VM = pl.BlockSpec(memory_space=pltpu.VMEM)


def dmas(*shape):
    return pltpu.SemaphoreType.DMA(shape)


def params(ident):
    return pltpu.CompilerParams(collective_id=ident, has_side_effects=True, vmem_limit_bytes=56 << 20)


def shape(*dims, dtype=BF16):
    return jax.ShapeDtypeStruct(dims, dtype)


SM = pl.BlockSpec(memory_space=pltpu.SMEM)


def shards(residual, targets, counts, enc_weight, enc_bias, dec_weight):
    n = GROUPS
    width = 2048 // n
    wide, thin = width // 2, width // 4
    goal = lax.dynamic_slice_in_dim(targets, lax.axis_index("loop") * 48, 48, 0).transpose(1, 0, 2)
    total_rows = 32 * 384 // 2
    vm = pltpu.VMEM
    dec_grad, enc_grad, bias_grad, loss = pl.pallas_call(
        lambda *refs: step_kernel(n, total_rows, *refs),
        out_shape=(
            shape(2, 64, 1024, dtype=F32), shape(32, 2048, dtype=F32), shape(16, 128, dtype=F32), shape(1, dtype=F32),
        ),
        in_specs=[SM, pl.BlockSpec(memory_space=pl.ANY), VM, pl.BlockSpec(memory_space=pl.ANY), VM, VM],
        out_specs=(VM, VM, VM, SM),
        scratch_shapes=[
            vm((2, 2, 32, 512), BF16), vm((1, 512), F32), vm((2, 2, 32, 512), F32), vm((2, 2, 8, 512), F32),
            vm((2, 2, 384, 1024), BF16), vm((2, 8, 2, 32, 512), BF16), vm((n, 8, 64, width), BF16),
            vm((1536, 512), F32), vm((1536, 512), BF16), vm((512, 1536), BF16), vm((1024, 1536), BF16),
            vm((n, width, 512), BF16),
            vm((n, 4, 4, 48, width), BF16), vm((n, 4, 4, 48, width), BF16), vm((n, 4, 4, 48, width), BF16),
            vm((n, 2, 4, 4, 48, width), BF16),
            vm((n, 2, 2, 2, 48, wide), BF16), vm((n, 2, 2, 4, 48, wide), BF16),
            vm((n, 2, 2, 48, thin), BF16), vm((n, 2, 2, 48, wide), BF16), vm((n, 2, 4, 48, wide), BF16),
            vm((1536, 512), F32), vm((1536, 512), BF16),
            vm((n, 8, 64, width), BF16), vm((2, 8, 2, 32, 512), BF16),
            vm((n, 2, 32, width), BF16), vm((n, 2, 3, 64, width), BF16),
            vm((2, 2, 32, 512), BF16), vm((2, 2, 3, 2, 32, 512), BF16), vm((2, 2, 32, 512), F32),
            vm((8, 128), F32), vm((4, 8, 128), F32), vm((4, 8, 128), F32), vm((2, 8, 128), F32),
            vm((8, 8, 640), F32), vm((8, 512), F32),
            dmas(2, 2, 2), dmas(2, 2, 2), dmas(2, 2, 2, 2), dmas(2, 2, 2), dmas(2, 2, 4), dmas(n, 2, 2, 4),
            dmas(2, 3), dmas(2, 2), dmas(n + 4), dmas(n, 2, 2), dmas(n, 2, 4, 2, 2, 2), dmas(n, 2, 2, 4),
            dmas(2, 2, 2), dmas(2, 2, 2), dmas(2), dmas(n, 2, 2, 4), dmas(2, 2, 2, 4), dmas(2, 2, 4),
            dmas(2, 3), dmas(2, 3),
        ],
        compiler_params=params(1),
    )(counts, residual, enc_weight, dec_weight.transpose(1, 0, 2), enc_bias.reshape(16, 128), goal)
    return loss.reshape(()), enc_grad, bias_grad.reshape(2048), dec_grad.transpose(1, 0, 2)


def solution(mesh):
    placed = (
        P("dp", "loop"),
        P("dp", None, None),
        P("dp"),
        P("dp", "loop"),
        P("loop"),
        P(("loop", "dp"), None, None),
    )
    return jax.shard_map(
        shards,
        mesh=mesh,
        in_specs=placed,
        out_specs=(P(), P("dp", "loop"), P("loop"), P(("loop", "dp"), None, None)),
        check_vma=False,
    )
```

```python
import math

import jax
import jax.numpy as jnp
from jax import lax
from jax.experimental import pallas as pl
from jax.experimental.pallas import tpu as pltpu
from jax.sharding import PartitionSpec as P

MESH = pl.DeviceIdType.MESH
BF16 = jnp.bfloat16
F32 = jnp.float32


def place():
    loop, dp = lax.axis_index("loop"), lax.axis_index("dp")
    x = (dp // 16) * 2 + loop // 4
    return x, loop % 4, (dp % 16) // 2, dp % 2


def ident(x, y, z, core):
    return ((x % 2) * 4 + y, (x // 2) * 16 + z * 2 + core)


def greet(peers):
    barrier = pltpu.get_barrier_semaphore()
    for peer in peers:
        pl.semaphore_signal(barrier, inc=1, device_id=peer, device_id_type=MESH)
    return lambda: pl.semaphore_wait(barrier, len(peers))


def remote(src, dst, send, recv, peer):
    return pltpu.make_async_remote_copy(
        src_ref=src, dst_ref=dst, send_sem=send, recv_sem=recv, device_id=peer, device_id_type=MESH
    )


class Gather:
    def __init__(self, n, at, right, left, whole, half, sems):
        self.n, self.at, self.right, self.left = n, at, right, left
        self.whole, self.half, self.sems = whole, half, sems
        self.steps = []

    def step(self):
        s = len(self.steps)
        if s:
            for copy in self.steps[-1]:
                copy.wait_recv()
        if s == self.n // 2:
            return
        pair = []
        for side, peer in ((0, self.right), (1, self.left)):
            block = (self.at + (self.n - s if side == 0 else s)) % self.n
            last = s == self.n // 2 - 1
            if last and self.half is None and side == 1:
                continue
            ref = self.half(block, side) if last and self.half is not None else self.whole(block)
            copy = remote(ref, ref, self.sems.at[0, side, s], self.sems.at[1, side, s], peer)
            copy.start()
            pair.append(copy)
        self.steps.append(pair)

    def drain(self):
        for pair in self.steps:
            for copy in pair:
                copy.wait_send()


def add_into(ref, other):
    ref[...] = (ref[...].astype(F32) + other[...].astype(F32)).astype(BF16)


class Reduce:
    def __init__(self, n, at, right, left, whole, half, landed, sems):
        self.n, self.at, self.right, self.left = n, at, right, left
        self.whole, self.half, self.landed, self.sems = whole, half, landed, sems
        self.steps = []

    def step(self):
        s = len(self.steps)
        depth = self.n // 2
        pair = []
        for side, peer in ((0, self.right), (1, self.left)):
            if s:
                self.steps[-1][side].wait_recv()
            if s == depth:
                continue
            far = depth - s
            block = (self.at + (far if side == 0 else self.n - far)) % self.n
            if s:
                part = self.half(block, side) if s == 1 else self.whole(block)
                add_into(part, self.landed[side][s - 1])
            ref = self.half(block, side) if s == 0 else self.whole(block)
            copy = remote(ref, self.landed[side][s], self.sems.at[0, side, s], self.sems.at[1, side, s], peer)
            copy.start()
            pair.append(copy)
        if s < depth:
            self.steps.append(pair)

    def drain(self):
        for pair in self.steps:
            for copy in pair:
                copy.wait_send()


GROUPS = 4
ORDER = (
    "d01", "u1", "v1", "e1", "d21", "v2", "u2", "d02", "e2", "d11", "x1", "y1",
    "d03", "e3", "d12", "x2", "d31", "y2", "e4", "xw", "d13", "d22", "yw", "d04",
    "d32", "ew", "n0", "rw", "d14", "n1", "d23", "d0w", "o0", "f0", "d33", "d1w",
    "o1", "d24", "m0", "p010", "p000", "d34", "m1", "p110", "d2w", "p100", "o2", "p011",
    "p001", "d3w", "o3", "p111", "p101", "m2", "p200", "p210", "m3", "p310", "p300", "p002",
    "p012", "p112", "p102", "p211", "p201", "ff", "p003", "p013", "p311", "p301", "f1", "p103",
    "p113", "f2", "p212", "p202", "p014", "p004", "fl", "p312", "p302", "p203", "p114", "p104",
    "p015", "p213", "p005", "p313", "p303", "p204", "p115", "p105", "p016", "p214", "p006", "p304",
    "p314", "p116", "s1", "p106", "f3", "p017", "p215", "p205", "p007", "p315", "p305", "s2",
    "p117", "p107", "p018", "p216", "p206", "p306", "p008", "p019", "p316", "s3", "p118", "p108",
    "p009", "D0", "r01", "p119", "p109", "p217", "D1", "p207", "r11", "p317", "r02", "A",
    "r12", "p208", "p218", "p307", "s4", "p318", "r03", "p209", "p219", "D2", "r21", "r13",
    "p319", "p308", "C", "r04", "p309", "r22", "B", "r14", "s5", "E0", "q01", "s6",
    "b1", "r23", "E1", "q11", "q02", "b2", "D3", "r31", "q12", "r0w", "r1w", "q03",
    "b3", "r32", "q13", "q04", "r33", "b4", "q14", "r24", "q0w", "r34", "q1w", "bw",
    "r2w", "r3w",
)


def dot(a, b, dims=((1,), (0,))):
    return lax.dot_general(a, b, (dims, ((), ())), preferred_element_type=F32)


def step_kernel(
    groups, total_rows, counts, res, enc_in, dec, bias_in, goal, dec_out, enc_grad, bias_grad, loss,
    enc, bias, enc_out, bias_out, res_all, enc_all, dec_all, pre, active, act_t, res_t, dec_t, sent, crossed, mine, grads,
    far1, far2, near1, near2, mid, back, narrow, dec_prod, enc_prod,
    dr1, drn, er1, ern, esum, squares, sq_y, sq_x, sq_c, small, small_sum,
    usem, vsem, ysem, xsem, esem, dsem, qsem, csem, lsem, psem, bsem, osem, sysem, sxsem, scsem,
    dsem2, esem2, msem, q2sem, q3sem,
):
    width = 2048 // groups
    wide, thin = width // 2, width // 4
    scale = 2.0 / math.sqrt(total_rows)
    x, y, z, core = place()
    x_hi = x // 2
    up, down = ident(x, y, (z + 1) % 8, core), ident(x, y, (z + 7) % 8, core)
    east, west = ident((x + 1) % 4, y, z, core), ident((x + 3) % 4, y, z, core)
    north, south = ident(x, (y + 1) % 4, z, core), ident(x, (y + 3) % 4, z, core)
    other = ident(x, y, z, 1 - core)
    quad = [(1 - x_hi, core), (x_hi, 1 - core), (1 - x_hi, 1 - core)]
    quad_ids = [ident((x + 2) % 4, y, z, core), other, ident((x + 2) % 4, y, z, 1 - core)]
    all_here = greet([up, down, east, west, north, south] + quad_ids)
    drains = []

    def cols(block, width):
        return pl.ds(pl.multiple_of(block * width, width), width)

    top, low = pl.ds(0, 192), pl.ds(192, 192)

    def feature(rows, xx, yy):
        return res_all.at[core, xx // 2, rows, cols((xx % 2) * 4 + yy, 128)]

    def feature_row(rows, xx):
        return res_all.at[core, xx // 2, rows, cols(xx % 2, 512)]

    def feature_both(rows, k, yy):
        return res_all.at[core, :, rows, cols(k * 4 + yy, 128)]

    def column(g):
        return divmod(g * width, 1024)

    local = [pltpu.make_async_copy(res, feature(pl.ds(0, 384), x, y), lsem.at[0])]
    for g in range(groups):
        t, at = column(g)
        local.append(pltpu.make_async_copy(dec.at[t, :, pl.ds(at, width)], dec_all.at[g, z], lsem.at[2 + g]))
    for copy in local:
        copy.start()
    runs = [(h, c, k, 1024 * h + 128 * k + 64 * c) for h in range(2) for c in range(2) for k in range(8)]
    for h, c, k, at in runs:
        enc[h, c, :, 64 * k : 64 * k + 64] = enc_in[:, at : at + 64]
    local.append(pltpu.make_async_copy(enc.at[x_hi, core], enc_all.at[x_hi, z, core], lsem.at[1]))
    local[-1].start()
    both = bias_in[pl.ds(pl.multiple_of(8 * x_hi, 8), 8), :]
    chosen = jnp.where(core == 0, both[:, 0:64], both[:, 64:128])
    for k in range(8):
        bias[:, 64 * k : 64 * k + 64] = chosen[k : k + 1, :]
    all_here()
    swap = []
    for i, (q, peer) in enumerate(zip(quad, quad_ids)):
        copy = remote(enc.at[q[0], q[1]], enc_all.at[x_hi, z, core], qsem.at[0, i], qsem.at[1, i], peer)
        copy.start()
        swap.append(copy)
    for copy in local:
        copy.wait()
    ring_e = Gather(8, z, up, down, lambda b: enc_all.at[:, b], lambda b, h: enc_all.at[h, b], esem)
    ring_d = [
        Gather(
            8, z, up, down, lambda b, t=t: dec_all.at[t, b],
            lambda b, h, t=t: dec_all.at[t, b, pl.ds(32 * h, 32)], dsem.at[t],
        )
        for t in range(groups)
    ]
    ring_u = Gather(
        4, y, north, south, lambda b: feature(top, x, b), lambda b, h: feature(pl.ds(96 * h, 96), x, b), usem
    )
    ring_v = Gather(
        4, x, east, west, lambda b: feature(low, b, y), lambda b, h: feature(pl.ds(192 + 96 * h, 96), b, y), vsem
    )
    ring_x = Gather(
        4, x, east, west, lambda b: feature_row(top, b), lambda b, h: feature_row(pl.ds(96 * h, 96), b), xsem
    )
    ring_y = [
        Gather(
            4, y, north, south, lambda b, k=k: feature_both(low, k, b),
            lambda b, h, k=k: feature_both(pl.ds(192 + 96 * h, 96), k, b), ysem.at[k],
        )
        for k in range(2)
    ]
    drains += [ring_u, ring_v, ring_x, ring_e] + ring_y + ring_d

    tasks = {"e1": lambda: ([copy.wait_recv() for copy in swap], ring_e.step())}

    def put(*names):
        def bind(action):
            for name in names:
                tasks[name] = action
            return action

        return bind

    for name in ("e2", "e3", "e4", "ew"):
        tasks[name] = ring_e.step
    for g in range(groups):
        for name in "1234w":
            tasks[f"d{g}{name}"] = ring_d[g].step
    for name in ("u1", "u2"):
        tasks[name] = ring_u.step
    for name in ("v1", "v2"):
        tasks[name] = ring_v.step
    cross = []

    def cross_over(i, rows):
        ref = res_all.at[core, :, rows]
        cross.append(remote(ref, ref, csem.at[i, 0], csem.at[i, 1], other))
        cross[-1].start()

    tasks["x1"] = lambda: (ring_u.step(), ring_x.step())
    tasks["x2"] = ring_x.step
    tasks["xw"] = lambda: (ring_x.step(), cross_over(0, top))
    tasks["y1"] = lambda: (ring_v.step(), ring_y[0].step(), ring_y[1].step())
    tasks["y2"] = lambda: (ring_y[0].step(), ring_y[1].step())
    tasks["yw"] = lambda: (ring_y[0].step(), ring_y[1].step(), cross_over(1, low))
    tasks["rw"] = lambda: [copy.wait_recv() for copy in cross]

    def encode(k, _):
        i = (2 * core + k) % 4
        rows = pl.ds(pl.multiple_of(384 * i, 384), 384)
        value = dot(res_all[i // 2, i % 2], enc_all[...].reshape(1024, 512)) + bias[...]
        pre[rows, :] = value
        active[rows, :] = jnp.maximum(value, 0.0).astype(BF16)
        return 0

    tasks["n0"] = lambda: lax.fori_loop(0, 2, encode, 0)
    tasks["n1"] = lambda: lax.fori_loop(2, 4, encode, 0)

    def flip_features(i, _):
        res_t[:, cols(i, 384)] = res_all[i // 2, i % 2].T
        return 0

    def flip_latents(i, _):
        act_t[:, cols(i, 384)] = active[pl.ds(pl.multiple_of(384 * i, 384), 384), :].T
        return 0

    def flip_decoder(g):
        def one(i, _):
            dec_t[g, :, cols(i, 128)] = dec_all[g, pl.ds(2 * i, 2)].reshape(128, width).T
            return 0

        lax.fori_loop(0, 4, one, 0)

    tasks["ff"] = lambda: lax.fori_loop(0, 4, flip_features, 0)
    tasks["fl"] = lambda: lax.fori_loop(0, 4, flip_latents, 0)

    def latent_rows(c, i):
        return pl.ds(pl.multiple_of(768 * c + 384 * i, 384), 384)

    def decode(g, c, i):
        return dot(active[latent_rows(c, i), :], dec_all[g].reshape(512, width)).reshape(2, 4, 48, width)

    def hand(g, i):
        pair = pl.ds(2 * i, 2)
        return remote(sent.at[g, pair], crossed.at[g, pair], psem.at[g, 0, i], psem.at[g, 1, i], other)

    def decode_other(g):
        def one(i, _):
            sent[g, pl.ds(2 * i, 2)] = decode(g, 1 - core, i).astype(BF16)
            hand(g, i).start()
            return 0

        lax.fori_loop(0, 2, one, 0)

    def decode_mine(g):
        def one(i, _):
            value = decode(g, core, i)
            hand(g, i).wait_recv()
            pair = pl.ds(2 * i, 2)
            mine[g, pair] = (value + crossed[g, pair].astype(F32)).astype(BF16)
            return 0

        lax.fori_loop(0, 2, one, 0)

    row = ((x % 2) * 4 + y) * 48 + lax.broadcasted_iota(jnp.int32, (48, 128), 0)
    ok = (row < counts[0]).astype(F32)[:, 0:1]
    along_x, along_y = (4, x, east, west), (4, y, north, south)
    squares[...] = jnp.zeros_like(squares)

    def exchange(g, q):
        own, out = mine.at[g], grads.at[g, core]
        t, start = column(g)
        w = pl.ds(q * wide, wide)
        first, then = (along_x, along_y) if q == 0 else (along_y, along_x)
        at, near = first[1], then[1]

        def lane(ref, b):
            return ref.at[b, :, :, w] if q == 0 else ref.at[:, b, :, w]

        def half_lane(ref, b, h):
            pair = pl.ds(2 * h, 2)
            return ref.at[b, pair, :, w] if q == 0 else ref.at[pair, b, :, w]

        def cell(b, where):
            return out.at[x, b, :, where] if q == 0 else out.at[b, y, :, where]

        def part(h):
            return pl.ds(q * wide + thin * h, thin)

        sems = bsem.at[g, q]
        red_far = Reduce(
            *first, lambda b: lane(own, b), lambda b, h: half_lane(own, b, h),
            [[far1.at[g, q, s], far2.at[g, q, s]] for s in range(2)], sems.at[0],
        )
        red_near = Reduce(
            *then, lambda b: mid.at[g, q, b], lambda b, h: mid.at[g, q, b, :, pl.ds(thin * h, thin)],
            [[near1.at[g, q, s], near2.at[g, q, s]] for s in range(2)], sems.at[1],
        )
        ring_near = Gather(*then, lambda b: cell(b, w), lambda b, h: cell(b, part(h)), sems.at[2])
        ring_far = Gather(*first, lambda b: lane(out, b), lambda b, h: half_lane(out, b, h), sems.at[3])
        drains.extend([red_far, red_near, ring_near, ring_far])
        over = []

        def hand_over(k):
            ref = lane(out, (at + k) % 4)
            over.append(remote(ref, ref, osem.at[g, q, 0, k], osem.at[g, q, 1, k], other))
            over[-1].start()

        red_far.step()
        yield
        red_far.step()
        yield
        red_far.step()
        mid[g, q] = (
            lane(own, at)[...].astype(F32) + far2[g, q, 0].astype(F32) + far2[g, q, 1].astype(F32)
        ).astype(BF16)
        red_near.step()
        yield
        red_near.step()
        yield
        red_near.step()
        rebuilt = mid[g, q, near].astype(F32) + near2[g, q, 0].astype(F32) + near2[g, q, 1].astype(F32)
        miss = (rebuilt - goal[t, :, pl.ds(start + q * wide, wide)].astype(F32)) * ok
        cell(near, w)[...] = (scale * miss).astype(BF16)
        ring_near.step()
        square = miss * miss
        parts = [
            square[8 * i : 8 * i + 8, 128 * j : 128 * j + 128] for i in range(6) for j in range(wide // 128)
        ]
        squares[...] += sum(parts[1:], parts[0])
        yield
        ring_near.step()
        yield
        ring_near.step()
        ring_far.step()
        hand_over(0)
        yield
        ring_far.step()
        hand_over(1)
        hand_over(3)
        yield
        ring_far.step()
        hand_over(2)
        yield
        for copy in over:
            copy.wait()
        yield

    def decoder_product(g):
        value = dot(act_t[...], grads[g].reshape(1536, width))
        dec_prod[g] = value.astype(BF16).reshape(8, 64, width)

    def finish_decoder(g, ring):
        ring.step()
        t, at = column(g)
        dec_out[t, :, at : at + width] = dec_prod[g, z].astype(F32) + drn[g, 0, 2].astype(F32) + drn[g, 1, 2].astype(F32)

    for g in range(groups):
        tasks[f"o{g}"] = lambda g=g: decode_other(g)
        tasks[f"m{g}"] = lambda g=g: decode_mine(g)
        tasks[f"f{g}"] = lambda g=g: flip_decoder(g)
        for q in range(2):
            flow = exchange(g, q)
            for k in range(10):
                tasks[f"p{g}{q}{k}"] = lambda flow=flow: next(flow)
        ring = Reduce(
            8, z, up, down, lambda b, g=g: dec_prod.at[g, b],
            lambda b, h, g=g: dec_prod.at[g, b, pl.ds(32 * h, 32)],
            [[dr1.at[g, s]] + [drn.at[g, s, i] for i in range(3)] for s in range(2)], dsem2.at[g],
        )
        drains.append(ring)
        tasks[f"D{g}"] = lambda g=g: decoder_product(g)
        for k in range(1, 5):
            tasks[f"r{g}{k}"] = ring.step
        tasks[f"r{g}w"] = lambda g=g, ring=ring: finish_decoder(g, ring)

    sum_y = Gather(*along_y, lambda b: sq_y.at[b], None, sysem)
    sum_x = Gather(*along_x, lambda b: sq_x.at[b], None, sxsem)
    sum_c = remote(sq_c.at[core], sq_c.at[core], scsem.at[0], scsem.at[1], other)
    drains += [sum_y, sum_x]
    tasks["s2"] = sum_y.step
    tasks["s4"] = sum_x.step

    @put("s1")
    def _():
        sq_y[y] = squares[...]
        sum_y.step()

    @put("s3")
    def _():
        sum_y.step()
        sq_x[x] = (sq_y[0] + sq_y[1]) + (sq_y[2] + sq_y[3])
        sum_x.step()

    @put("s5")
    def _():
        sum_x.step()
        sq_c[core] = (sq_x[0] + sq_x[1]) + (sq_x[2] + sq_x[3])
        sum_c.start()

    @put("s6")
    def _():
        sum_c.wait()
        small[z, :, 512:640] = sq_c[0] + sq_c[1]

    def spread(some, c, i):
        terms = [dot(grads[g, c, pl.ds(2 * i, 2)].reshape(384, width), dec_t[g]) for g in some]
        return sum(terms[1:], terms[0])

    def spread_first(i, _):
        back[latent_rows(i // 2, i % 2), :] = spread(range(groups - 2), i // 2, i % 2)
        return 0

    def spread_next(i, _):
        back[latent_rows(i // 2, i % 2), :] += spread((groups - 2,), i // 2, i % 2)
        return 0

    def spread_last(i, total):
        rows = latent_rows(i // 2, i % 2)
        value = back[rows, :] + spread((groups - 1,), i // 2, i % 2)
        value = jnp.where(pre[rows, :] > 0, value, 0.0)
        narrow[rows, :] = value.astype(BF16)
        return total + jnp.sum(value.reshape(48, 8, 512), axis=0)

    tasks["A"] = lambda: lax.fori_loop(0, 4, spread_first, 0)
    tasks["C"] = lambda: lax.fori_loop(0, 4, spread_next, 0)

    @put("B")
    def _():
        small[z, :, 0:512] = lax.fori_loop(0, 4, spread_last, jnp.zeros((8, 512), F32))

    ring_m = Gather(8, z, up, down, lambda b: small.at[b], None, msem)
    drains.append(ring_m)
    for k in range(1, 5):
        tasks[f"b{k}"] = ring_m.step
    keep = []

    @put("bw")
    def _():
        ring_m.step()
        full = ((small[0] + small[1]) + (small[2] + small[3])) + ((small[4] + small[5]) + (small[6] + small[7]))
        loss[0] = jnp.sum(full[:, 512:640]) / (total_rows * 2048)
        small_sum[...] = full[:, 0:512]
        keep.append(pltpu.make_async_copy(small_sum, bias_out.at[x_hi, core], lsem.at[2 + groups]))
        keep[-1].start()
        for i, peer in enumerate(quad_ids):
            copy = remote(small_sum, bias_out.at[x_hi, core], q3sem.at[0, i], q3sem.at[1, i], peer)
            copy.start()
            keep.append(copy)

    def encoder_product(i, side):
        value = dot(res_t[pl.ds(pl.multiple_of(512 * side, 512), 512), :], narrow[...])
        enc_prod[side] = value.astype(BF16).reshape(8, 2, 32, 512)

    def finish_encoder(i, side, ring):
        ring.step()
        esum[side] = enc_prod[side, z].astype(F32) + ern[i, 0, 2].astype(F32) + ern[i, 1, 2].astype(F32)
        for j, (q, peer) in enumerate(zip(quad, quad_ids)):
            if (j == 1) == (i == 1):
                copy = remote(esum.at[q[0], q[1]], enc_out.at[x_hi, core], q2sem.at[0, j], q2sem.at[1, j], peer)
                copy.start()
                keep.append(copy)
        if i == 1:
            keep.append(pltpu.make_async_copy(esum.at[x_hi, core], enc_out.at[x_hi, core], lsem.at[3 + groups]))
            keep[-1].start()

    for i, side in enumerate((1 - x_hi, x_hi)):
        ring = Reduce(
            8, z, up, down, lambda b, side=side: enc_prod.at[side, b],
            lambda b, h, side=side: enc_prod.at[side, b, h],
            [[er1.at[i, s]] + [ern.at[i, s, k] for k in range(3)] for s in range(2)], esem2.at[i],
        )
        drains.append(ring)
        tasks[f"E{i}"] = lambda i=i, side=side: encoder_product(i, side)
        for k in range(1, 5):
            tasks[f"q{i}{k}"] = ring.step
        tasks[f"q{i}w"] = lambda i=i, side=side, ring=ring: finish_encoder(i, side, ring)

    for name in ORDER:
        tasks[name]()
    for copy in keep:
        copy.wait()
    sums = [[jnp.sum(bias_out[h, c], axis=0, keepdims=True) for c in range(2)] for h in range(2)]
    for h, c, k, at in runs:
        enc_grad[:, at : at + 64] = enc_out[h, c, :, 64 * k : 64 * k + 64]
        bias_grad[8 * h + k : 8 * h + k + 1, 64 * c : 64 * c + 64] = sums[h][c][:, 64 * k : 64 * k + 64]
    for copy in swap + cross:
        copy.wait_send()
    for g in range(groups):
        for i in range(2):
            hand(g, i).wait_send()
    for ring in drains:
        ring.drain()


VM = pl.BlockSpec(memory_space=pltpu.VMEM)


def dmas(*shape):
    return pltpu.SemaphoreType.DMA(shape)


def params(ident):
    return pltpu.CompilerParams(collective_id=ident, has_side_effects=True, vmem_limit_bytes=56 << 20)


def shape(*dims, dtype=BF16):
    return jax.ShapeDtypeStruct(dims, dtype)


SM = pl.BlockSpec(memory_space=pltpu.SMEM)


def shards(residual, targets, counts, enc_weight, enc_bias, dec_weight):
    n = GROUPS
    width = 2048 // n
    wide, thin = width // 2, width // 4
    goal = lax.dynamic_slice_in_dim(targets, lax.axis_index("loop") * 48, 48, 0).transpose(1, 0, 2)
    total_rows = 32 * 384 // 2
    vm = pltpu.VMEM
    dec_grad, enc_grad, bias_grad, loss = pl.pallas_call(
        lambda *refs: step_kernel(n, total_rows, *refs),
        out_shape=(
            shape(2, 64, 1024, dtype=F32), shape(32, 2048, dtype=F32), shape(16, 128, dtype=F32), shape(1, dtype=F32),
        ),
        in_specs=[SM, pl.BlockSpec(memory_space=pl.ANY), VM, pl.BlockSpec(memory_space=pl.ANY), VM, VM],
        out_specs=(VM, VM, VM, SM),
        scratch_shapes=[
            vm((2, 2, 32, 512), BF16), vm((1, 512), F32), vm((2, 2, 32, 512), F32), vm((2, 2, 8, 512), F32),
            vm((2, 2, 384, 1024), BF16), vm((2, 8, 2, 32, 512), BF16), vm((n, 8, 64, width), BF16),
            vm((1536, 512), F32), vm((1536, 512), BF16), vm((512, 1536), BF16), vm((1024, 1536), BF16),
            vm((n, width, 512), BF16),
            vm((n, 4, 4, 48, width), BF16), vm((n, 4, 4, 48, width), BF16), vm((n, 4, 4, 48, width), BF16),
            vm((n, 2, 4, 4, 48, width), BF16),
            vm((n, 2, 2, 2, 48, wide), BF16), vm((n, 2, 2, 4, 48, wide), BF16),
            vm((n, 2, 2, 48, thin), BF16), vm((n, 2, 2, 48, wide), BF16), vm((n, 2, 4, 48, wide), BF16),
            vm((1536, 512), F32), vm((1536, 512), BF16),
            vm((n, 8, 64, width), BF16), vm((2, 8, 2, 32, 512), BF16),
            vm((n, 2, 32, width), BF16), vm((n, 2, 3, 64, width), BF16),
            vm((2, 2, 32, 512), BF16), vm((2, 2, 3, 2, 32, 512), BF16), vm((2, 2, 32, 512), F32),
            vm((8, 128), F32), vm((4, 8, 128), F32), vm((4, 8, 128), F32), vm((2, 8, 128), F32),
            vm((8, 8, 640), F32), vm((8, 512), F32),
            dmas(2, 2, 2), dmas(2, 2, 2), dmas(2, 2, 2, 2), dmas(2, 2, 2), dmas(2, 2, 4), dmas(n, 2, 2, 4),
            dmas(2, 3), dmas(2, 2), dmas(n + 4), dmas(n, 2, 2), dmas(n, 2, 4, 2, 2, 2), dmas(n, 2, 2, 4),
            dmas(2, 2, 2), dmas(2, 2, 2), dmas(2), dmas(n, 2, 2, 4), dmas(2, 2, 2, 4), dmas(2, 2, 4),
            dmas(2, 3), dmas(2, 3),
        ],
        compiler_params=params(1),
    )(counts, residual, enc_weight, dec_weight.transpose(1, 0, 2), enc_bias.reshape(16, 128), goal)
    return loss.reshape(()), enc_grad, bias_grad.reshape(2048), dec_grad.transpose(1, 0, 2)


def solution(mesh):
    placed = (
        P("dp", "loop"),
        P("dp", None, None),
        P("dp"),
        P("dp", "loop"),
        P("loop"),
        P(("loop", "dp"), None, None),
    )
    return jax.shard_map(
        shards,
        mesh=mesh,
        in_specs=placed,
        out_specs=(P(), P("dp", "loop"), P("loop"), P(("loop", "dp"), None, None)),
        check_vma=False,
    )
```
